32 devices in a mesh: parts: 2 (over y), replica: 4 (over x, core), tensor: 4 (over z).
Axes of the slice: x: 2, y: 2, z: 4, core: 2. Of those that a mesh axis runs over, the one named last changes fastest.
Arguments:
- embedded: bfloat16 [8, 128, 5120], P(None, ('parts', 'replica'), 'tensor'), parts along dimension 1, may hold values from -500 to 500
- w_query: bfloat16 [5120, 4096], P(None, 'tensor'), may hold values from -0.078125 to 0.078125
- w_key: bfloat16 [5120, 512], P(None, 'tensor'), may hold values from -0.078125 to 0.078125
- w_value: bfloat16 [5120, 512], P(None, 'tensor'), may hold values from -0.078125 to 0.078125
- w_out: bfloat16 [4096, 5120], P(None, 'tensor'), may hold values from -0.09375 to 0.09375
- prefix_cache: bfloat16 [32, 2048, 1024], P(('parts', 'replica'), 'tensor'), parts along dimension 0, may hold values from -70 to 70
- prefix_len: int32 [32], P(('parts', 'replica')), parts along dimension 0, may hold values from 1 to 2048, as said below
- child_parent: int32 [128], P(('parts', 'replica')), parts along dimension 0, may hold values from 0 to 15, as said below
Outputs:
- attn_out: bfloat16 [8, 128, 5120], P(None, ('parts', 'replica'), 'tensor'), parts along dimension 1
The draws below stay inside these ranges and needn't reach their ends.
There are 2 independent parts, one for each index of `parts`. The reference program is written for one: setup_inputs(seed, part) draws one part's arguments, and reference() takes and returns one part's arrays. A program takes and returns all parts, laid end to end along the dimension named above; an argument that names none is the same for every part. Nothing has to cross between parts.
Inputs may be any that keep to these rules, and one draw needn't show every extreme that they name: `child_parent`: parent p lives on replica p // 4; every child slot names a parent on another replica; the child slots of one replica name exactly 2 distinct parents of each other replica. `prefix_len`: one parent in every part has the full 2048.
All inputs are finite; a program needn't handle non-finite values.
Results may differ from the reference program's by a relative error of at most 0.025.
Values may be sent and summed in bfloat16 or wider, within the bound.
A program may use at most 320 MiB of HBM per device.

```python
import math
import jax
import jax.numpy as jnp
from jax import lax

D = 5120
HEADS = 32
KV_HEADS = 4
HEAD = 128
PREFIX = 2048
STEPS = 8
PAR_REP = 4
CAP = 2
CHILD_REP = 16
PARENTS = 16
CHILDREN = 64


def draw_embedded(key, part):
    key = jax.random.fold_in(key, 5)
    first, second, third = jax.random.split(key, 3)
    shape = (STEPS, CHILDREN, D)
    base = jnp.clip(jax.random.normal(first, shape, jnp.float32), -5.0, 5.0)
    row_scale = jnp.exp(jax.random.uniform(second, (STEPS, CHILDREN, 1), jnp.float32) * math.log(10.0))
    col_scale = jnp.exp(jax.random.uniform(third, (1, 1, D), jnp.float32) * math.log(10.0))
    return (base * row_scale * col_scale).astype(jnp.bfloat16)


def draw_prefix_cache(key, part):
    key = jax.random.fold_in(key, 7)
    first = jax.random.fold_in(key, 0)
    width = 2 * KV_HEADS * HEAD
    shape = (PARENTS, PREFIX, width)
    column_scale = jnp.where(jnp.arange(width) < KV_HEADS * HEAD, 1.0, 8.0).astype(jnp.float32)
    base = jnp.clip(jax.random.normal(first, shape, jnp.float32), -5.0, 5.0) * column_scale
    return base.astype(jnp.bfloat16)


def draw_prefix_len(key, part):
    key = jax.random.fold_in(key, 9)
    first, second = jax.random.split(key, 2)
    lengths = jax.random.randint(first, (PARENTS,), 1, PREFIX + 1)
    longest = jax.random.randint(second, (), 0, PARENTS)
    lengths = jnp.where(jnp.arange(PARENTS) == longest, PREFIX, lengths)
    return lengths.astype(jnp.int32)


def draw_child_parent(key, part):
    key = jax.random.fold_in(key, 11)
    replicas = PARENTS // PAR_REP
    slots = jnp.arange(CHILDREN, dtype=jnp.int32)
    target = slots // CHILD_REP
    within = slots % CHILD_REP
    source = (target + 1 + within % (replicas - 1)) % replicas
    turn = within // (replicas - 1)
    pair_keys = jax.random.split(jax.random.fold_in(key, 1), replicas * replicas)
    orders = jax.vmap(lambda one: jax.random.permutation(one, PAR_REP))(pair_keys).reshape(replicas, replicas, PAR_REP)
    extra = jax.random.randint(jax.random.fold_in(key, 2), (CHILDREN,), 0, CAP)
    which = jnp.where(turn < CAP, turn, extra)
    local = orders[target, source, which]
    return (source * PAR_REP + local).astype(jnp.int32)


def steps_of(own_key, shape, pieces, low, top_value):
    gain, own = 1.0, jax.random.fold_in(own_key, 6)
    for dim, parts in pieces:
        draws = jnp.exp(jax.random.uniform(jax.random.fold_in(own, dim), (parts,), jnp.float32, low / len(pieces), top_value / len(pieces)))
        gain = gain * jnp.repeat(draws, shape[dim] // parts).reshape([-1 if axis == dim else 1 for axis in range(len(shape))])
    return gain


def gaussian(rng, shape, spread, reach, cuts=(), kind=jnp.bfloat16):
    entries = spread * jax.random.normal(rng, shape, jnp.float32)
    if cuts:
        entries = entries * steps_of(rng, shape, cuts, -0.22, 0.18)
    return jnp.clip(entries, -reach, reach).astype(kind)


def setup_inputs(seed: int = 0, part: int = 0) -> dict:
    streams_of = jax.random.split(jax.random.key(seed), 9)
    part_splits = jax.random.split(jax.random.fold_in(streams_of[8], part), 9)
    return {
        "embedded": draw_embedded(jax.random.fold_in(jax.random.fold_in(streams_of[8], part), 71), part),
        "w_query": gaussian(streams_of[1], (D, HEADS * HEAD), D ** -0.5, 0.078125, ((1, 4),)),
        "w_key": gaussian(streams_of[2], (D, KV_HEADS * HEAD), D ** -0.5, 0.078125, ((1, 4),)),
        "w_value": gaussian(streams_of[3], (D, KV_HEADS * HEAD), D ** -0.5, 0.078125, ((1, 4),)),
        "w_out": gaussian(streams_of[4], (HEADS * HEAD, D), (HEADS * HEAD) ** -0.5, 0.09375, ((1, 4),)),
        "prefix_cache": draw_prefix_cache(jax.random.fold_in(jax.random.fold_in(streams_of[8], part), 71), part),
        "prefix_len": draw_prefix_len(jax.random.fold_in(jax.random.fold_in(streams_of[8], part), 71), part),
        "child_parent": draw_child_parent(jax.random.fold_in(jax.random.fold_in(streams_of[8], part), 71), part),
    }


EPS = 1e-06
NEG = -1e+30
ROPE_BASE = 1000000.0

def rotate(values, positions):
    half = values.shape[-1] // 2
    freq = ROPE_BASE ** (-jnp.arange(half, dtype=jnp.float32) / half)
    angle = positions.astype(jnp.float32)[..., None] * freq
    cosine = jnp.cos(angle)
    sine = jnp.sin(angle)
    first = values[..., :half]
    second = values[..., half:]
    return jnp.concatenate([first * cosine - second * sine, first * sine + second * cosine], axis=-1)

def reference(embedded, w_query, w_key, w_value, w_out, prefix_cache, prefix_len, child_parent):
    kv_width = KV_HEADS * HEAD
    group = HEADS // KV_HEADS
    scale = HEAD ** (-0.5)
    whole = embedded.astype(jnp.float32)
    normed = (whole * lax.rsqrt(lax.optimization_barrier(jnp.mean(whole * whole, axis=-1, keepdims=True)) + EPS)).astype(jnp.bfloat16)
    flat = normed.reshape(STEPS * CHILDREN, D)
    lengths = prefix_len[child_parent]
    position = lengths[None, :] + jnp.arange(STEPS, dtype=jnp.int32)[:, None]
    query = jnp.dot(flat, w_query, preferred_element_type=jnp.float32).reshape(STEPS, CHILDREN, HEADS, HEAD)
    query = rotate(query, position[:, :, None]).astype(jnp.bfloat16)
    key_raw = jnp.dot(flat, w_key, preferred_element_type=jnp.float32).astype(jnp.bfloat16)
    key_new = rotate(key_raw.astype(jnp.float32).reshape(STEPS, CHILDREN, KV_HEADS, HEAD), position[:, :, None]).astype(jnp.bfloat16)
    value = jnp.dot(flat, w_value, preferred_element_type=jnp.float32).astype(jnp.bfloat16).reshape(STEPS, CHILDREN, KV_HEADS, HEAD)
    causal = jnp.arange(STEPS)[None, :] <= jnp.arange(STEPS)[:, None]

    def attend(child):
        parent = child_parent[child]
        cache = lax.dynamic_index_in_dim(prefix_cache, parent, 0, keepdims=False)
        keys = cache[:, :kv_width].reshape(PREFIX, KV_HEADS, HEAD).astype(jnp.float32)
        vals = cache[:, kv_width:].reshape(PREFIX, KV_HEADS, HEAD).astype(jnp.float32)
        queries = query[:, child].astype(jnp.float32).reshape(STEPS, KV_HEADS, group, HEAD)
        own_keys = key_new[:, child].astype(jnp.float32)
        own_vals = value[:, child].astype(jnp.float32)
        valid = jnp.arange(PREFIX) < lengths[child]
        pre = jnp.einsum('skgd,pkd->skgp', queries, keys) * scale
        pre = jnp.where(valid[None, None, None, :], pre, NEG)
        own = jnp.einsum('skgd,tkd->skgt', queries, own_keys) * scale
        own_mask = causal[:, None, None, :]
        own = jnp.where(own_mask, own, NEG)
        top = jnp.maximum(lax.optimization_barrier(jnp.max(pre, axis=-1)), lax.optimization_barrier(jnp.max(own, axis=-1)))
        pre_w = jnp.where(valid[None, None, None, :], jnp.exp(pre - top[..., None]), 0.0)
        own_w = jnp.where(own_mask, jnp.exp(own - top[..., None]), 0.0)
        total = lax.optimization_barrier(jnp.sum(pre_w, axis=-1)) + lax.optimization_barrier(jnp.sum(own_w, axis=-1))
        pre_b = lax.optimization_barrier(pre_w.astype(jnp.bfloat16)).astype(jnp.float32)
        own_b = lax.optimization_barrier(own_w.astype(jnp.bfloat16)).astype(jnp.float32)
        summed = jnp.einsum('skgp,pkd->skgd', pre_b, vals) + jnp.einsum('skgt,tkd->skgd', own_b, own_vals)
        return (summed / total[..., None]).reshape(STEPS, HEADS * HEAD)
    attended = lax.map(attend, jnp.arange(CHILDREN, dtype=jnp.int32))
    attended = jnp.transpose(attended, (1, 0, 2)).astype(jnp.bfloat16).reshape(STEPS * CHILDREN, HEADS * HEAD)
    result = jnp.dot(attended, w_out, preferred_element_type=jnp.float32).astype(jnp.bfloat16)
    return result.reshape(STEPS, CHILDREN, D)
```

```python
import functools

import jax
import jax.numpy as jnp
from jax import lax
from jax.experimental import pallas as pl
from jax.experimental.pallas import tpu as pltpu
from jax.sharding import PartitionSpec as P

HEADS = 32
KV_HEADS = 4
HEAD = 128


EPS = 1e-06
NEG = -1e30
ROPE_BASE = 1000000.0


def combined_all(x, axis, combine):
    everything = jax.tree.map(
        lambda part, kind: lax.all_gather(part.astype(kind), axis),
        x,
        (jnp.bfloat16, jnp.bfloat16, jnp.bfloat16),
    )

    def take(k):
        return jax.tree.map(lambda part, own: part[k].astype(own.dtype), everything, x)

    return lax.fori_loop(
        1, lax.axis_size(axis), lambda k, so_far: combine(so_far, take(k)), take(0)
    )


def rotate(values, positions):
    half = values.shape[-1] // 2
    freq = ROPE_BASE ** (-jnp.arange(half, dtype=jnp.float32) / half)
    angle = positions.astype(jnp.float32)[..., None] * freq
    cosine = jnp.cos(angle)
    sine = jnp.sin(angle)
    first = values[..., :half]
    second = values[..., half:]
    return jnp.concatenate(
        [first * cosine - second * sine, first * sine + second * cosine], axis=-1
    )


def combine(first, second):
    upper = jnp.maximum(first[0], second[0])
    left = jnp.exp(first[0] - upper)
    right = jnp.exp(second[0] - upper)
    return (
        upper,
        first[1] * left + second[1] * right,
        first[2] * left[..., None] + second[2] * right[..., None],
    )


def rms_normed(current):
    whole = current.astype(jnp.float32)
    return (whole * lax.rsqrt(jnp.mean(whole * whole, axis=-1, keepdims=True) + EPS)).astype(
        jnp.bfloat16
    )


def per_device(embedded, w_query, w_key, w_value, w_out, prefix_cache, prefix_len, child_parent):
    steps = embedded.shape[0]
    rows = embedded.shape[1]
    par_dev, pos_dev, width = prefix_cache.shape
    kv_width = width // 2
    group = HEADS // KV_HEADS
    scale = HEAD ** (-0.5)
    table = lax.all_gather(prefix_cache, "replica", axis=0, tiled=True)
    lengths_all = lax.all_gather(prefix_len, "replica", axis=0, tiled=True)
    lengths = lengths_all[child_parent]
    chosen = jnp.take(table, child_parent, axis=0)
    keys = jnp.transpose(
        chosen[:, :, :kv_width].reshape(rows, pos_dev, KV_HEADS, HEAD), (0, 2, 1, 3)
    )
    values = jnp.transpose(
        chosen[:, :, kv_width:].reshape(rows, pos_dev, KV_HEADS, HEAD), (0, 2, 1, 3)
    )
    positions = lax.axis_index("tensor") * pos_dev + jnp.arange(pos_dev, dtype=jnp.int32)
    valid = positions[None, :] < lengths[:, None]
    block_mask = valid[:, None, None, :]
    features = jnp.stack(
        [lax.all_gather(embedded[step], "tensor", axis=1, tiled=True) for step in range(steps)],
        axis=0,
    )
    normed = rms_normed(features).reshape(steps * rows, -1)
    position = lengths[None, :] + jnp.arange(steps, dtype=jnp.int32)[:, None]
    query_part = jnp.dot(normed, w_query, preferred_element_type=jnp.float32)
    local_heads = query_part.shape[1] // HEAD
    query_part = (
        rotate(query_part.reshape(steps, rows, local_heads, HEAD), position[:, :, None])
        .reshape(steps, rows, local_heads * HEAD)
        .astype(jnp.bfloat16)
    )
    key_part = (
        jnp.dot(normed, w_key, preferred_element_type=jnp.float32)
        .astype(jnp.bfloat16)
        .reshape(steps, rows, -1)
    )
    value_part = (
        jnp.dot(normed, w_value, preferred_element_type=jnp.float32)
        .astype(jnp.bfloat16)
        .reshape(steps, rows, -1)
    )
    query_all, key_all, value_all = (
        lax.all_gather(query_part, "tensor", axis=2, tiled=True),
        lax.all_gather(key_part, "tensor", axis=2, tiled=True),
        lax.all_gather(value_part, "tensor", axis=2, tiled=True),
    )
    own_keys = rotate(
        key_all.astype(jnp.float32).reshape(steps, rows, KV_HEADS, HEAD), position[:, :, None]
    ).astype(jnp.bfloat16)
    own_values = value_all.reshape(steps, rows, KV_HEADS, HEAD)
    queries = query_all.reshape(steps, rows, KV_HEADS, group, HEAD)
    scores = (
        jnp.einsum("sckgd,ckpd->sckgp", queries, keys, preferred_element_type=jnp.float32) * scale
    )
    full_mask = block_mask[None]
    scores = jnp.where(full_mask, scores, NEG)
    upper = jnp.max(scores, axis=-1)
    weights = jnp.where(full_mask, jnp.exp(scores - upper[..., None]), 0.0)
    total = jnp.sum(weights, axis=-1)
    partial_value = jnp.einsum(
        "sckgp,ckpd->sckgd",
        weights.astype(jnp.bfloat16),
        values,
        preferred_element_type=jnp.float32,
    )
    merged = combined_all((upper, total, partial_value), "tensor", combine)
    causal = (jnp.arange(steps)[None, :] <= jnp.arange(steps)[:, None])[:, None, None, None, :]
    own_scores = (
        jnp.einsum("sckgd,tckd->sckgt", queries, own_keys, preferred_element_type=jnp.float32)
        * scale
    )
    own_scores = jnp.where(causal, own_scores, NEG)
    own_upper = jnp.max(own_scores, axis=-1)
    own_weights = jnp.where(causal, jnp.exp(own_scores - own_upper[..., None]), 0.0)
    own_total = jnp.sum(own_weights, axis=-1)
    own_partial = jnp.einsum(
        "sckgt,tckd->sckgd",
        own_weights.astype(jnp.bfloat16),
        own_values,
        preferred_element_type=jnp.float32,
    )
    final = combine(merged, (own_upper, own_total, own_partial))
    attended = (
        (final[2] / final[1][..., None]).reshape(steps * rows, HEADS * HEAD).astype(jnp.bfloat16)
    )
    result = jnp.dot(attended, w_out, preferred_element_type=jnp.float32).astype(jnp.bfloat16)
    return result.reshape(steps, rows, -1)


GROUP = HEADS // KV_HEADS
SCALE = HEAD ** (-0.5)
MESH = pl.DeviceIdType.MESH


def flip(index, step):
    if step == 0:
        return index
    if step == 1:
        return index + 1 - 2 * lax.rem(index, 2)
    if step == 2:
        return index + 2 - 4 * (index // 2)
    return 3 - index


def send(src, dst, sems, slot, device):
    copy = pltpu.make_async_remote_copy(
        src_ref=src,
        dst_ref=dst,
        send_sem=sems[0].at[slot],
        recv_sem=sems[1].at[slot],
        device_id=device,
        device_id_type=MESH,
    )
    copy.start()
    return copy


def greet(devices):
    barrier = pltpu.get_barrier_semaphore()
    for device in devices:
        pl.semaphore_signal(barrier, inc=1, device_id=device, device_id_type=MESH)
    pl.semaphore_wait(barrier, len(devices))


def compact(column, children, rows):
    lane = lax.broadcasted_iota(jnp.int32, (rows, 128), 1)
    out = jnp.zeros((rows, 128), jnp.float32)
    for c in range(children):
        out = jnp.where(lane == c, column[c * rows : (c + 1) * rows], out)
    return out


def project_kernel(
    emb,
    meta,
    cpb,
    freq,
    wq,
    wk,
    wv,
    cache,
    q_own,
    q_part,
    kv_sib,
    meta_all,
    o_self,
    l_self,
    ebuf,
    wqb,
    wkb,
    accq,
    acck,
    qsend,
    e_s,
    e_r,
    w_s,
    q_s,
    q_r,
    x_s,
    x_r,
    m_s,
    m_r,
    k_s,
    k_r,
    loc_s,
):
    part = lax.axis_index("parts")
    r = lax.axis_index("replica")
    t = lax.axis_index("tensor")
    rows, width = emb.shape
    children = q_own.shape[1]
    steps = rows // children
    par_dev = cache.shape[0]

    def at(rep, ten):
        return (part, rep, ten)

    loads = []
    for d in range(4):
        k = flip(t, d)
        span = pl.ds(pl.multiple_of(k * width, width), width)
        loads.append(
            (
                pltpu.make_async_copy(wq.at[span], wqb.at[d], w_s.at[3 * d]),
                pltpu.make_async_copy(
                    wk.at[span], wkb.at[d, :, pl.ds(0, HEAD)], w_s.at[3 * d + 1]
                ),
                pltpu.make_async_copy(
                    wv.at[span], wkb.at[d, :, pl.ds(HEAD, HEAD)], w_s.at[3 * d + 2]
                ),
            )
        )
        for load in loads[-1]:
            load.start()
    own_meta = pltpu.make_async_copy(meta, meta_all.at[0], loc_s.at[0])
    own_meta.start()

    greet([at(r, flip(t, d)) for d in (1, 2, 3)] + [at(flip(r, d), t) for d in (1, 2, 3)])
    e_copies = [
        send(emb, ebuf.at[d - 1], (e_s, e_r), d - 1, at(r, flip(t, d))) for d in (1, 2, 3)
    ]
    m_copies = [
        send(meta, meta_all.at[d], (m_s, m_r), d - 1, at(flip(r, d), t)) for d in (1, 2, 3)
    ]
    kv_copy = send(cache, kv_sib, (k_s, k_r), 0, at(flip(r, 1), t))

    own_meta.wait()
    for copy in m_copies:
        copy.wait_recv()
    position = jnp.zeros((rows, 128), jnp.int32)
    parents = cpb[...]
    for d in range(4):
        rep = flip(r, d)
        table = meta_all[d]
        for i in range(par_dev):
            position = jnp.where(parents == rep * par_dev + i, table[i : i + 1, :], position)
    step = lax.rem(lax.broadcasted_iota(jnp.int32, (rows, 128), 0), steps)
    angle = (position + step).astype(jnp.float32) * freq[...]
    cosine = jnp.cos(angle)
    half = lax.broadcasted_iota(jnp.int32, (rows, 128), 1) < HEAD // 2
    sine = jnp.sin(angle)
    sine = jnp.where(half, -sine, sine)

    squares = jnp.zeros((rows, 1), jnp.float32)
    for d in range(4):
        if d:
            e_copies[d - 1].wait_recv()
        block = emb[...] if d == 0 else ebuf[d - 1]
        whole = block.astype(jnp.float32)
        squares = squares + jnp.sum(whole * whole, axis=-1, keepdims=True)
        for load in loads[d]:
            load.wait()
        more_q = jnp.dot(block, wqb[d], preferred_element_type=jnp.float32)
        more_k = jnp.dot(block, wkb[d], preferred_element_type=jnp.float32)
        if d == 0:
            accq[...] = more_q
            acck[...] = more_k
        else:
            accq[...] += more_q
            acck[...] += more_k
    norm = lax.rsqrt(squares / (4 * width) + EPS)

    def turn(x):
        return x * cosine + pltpu.roll(x, HEAD // 2, 1) * sine

    def head_of(g):
        x = turn(accq[:, g * HEAD : (g + 1) * HEAD] * norm)
        return x.reshape(children, steps, HEAD)

    for j in range(GROUP // 2):
        pair = jnp.concatenate([head_of(2 * j), head_of(2 * j + 1)], axis=1)
        qsend[:, 2 * steps * j : 2 * steps * (j + 1), :] = pair.astype(jnp.bfloat16)

    own_q = pltpu.make_async_copy(qsend, q_own.at[t], loc_s.at[1])
    own_q.start()
    z_copies = [
        send(qsend, q_own.at[t], (q_s, q_r), d - 1, at(r, flip(t, d))) for d in (1, 2, 3)
    ]
    x_copies = [send(qsend, q_part.at[t], (x_s, x_r), 0, at(flip(r, 2), t))]

    key_raw = (acck[:, :HEAD] * norm).astype(jnp.bfloat16).astype(jnp.float32)
    key_new = turn(key_raw).astype(jnp.bfloat16)
    value = (acck[:, HEAD:] * norm).astype(jnp.bfloat16)
    total_rows = children * GROUP * steps
    scores = (
        lax.dot_general(
            qsend[...].reshape(total_rows, HEAD),
            key_new,
            (((1,), (1,)), ((), ())),
            preferred_element_type=jnp.float32,
        )
        * SCALE
    )
    row = lax.broadcasted_iota(jnp.int32, (total_rows, rows), 0)
    col = lax.broadcasted_iota(jnp.int32, (total_rows, rows), 1)
    valid = (row // (GROUP * steps) == col // steps) & (lax.rem(col, steps) <= lax.rem(row, steps))
    scores = jnp.where(valid, scores, NEG)
    top = jnp.max(scores, axis=-1, keepdims=True)
    weights = jnp.where(valid, jnp.exp(scores - top), 0.0)
    total = jnp.sum(weights, axis=-1, keepdims=True)
    summed = jnp.dot(weights.astype(jnp.bfloat16), value, preferred_element_type=jnp.float32)
    o_self[...] = (summed / total).reshape(children, GROUP * steps, HEAD)
    l_self[...] = compact(top + jnp.log(total), children, GROUP * steps)

    for d in (1, 2, 3):
        z_copies[d - 1].wait_recv()
        k = flip(t, d)
        x_copies.append(
            send(q_own.at[k], q_part.at[k], (x_s, x_r), d, at(flip(r, 2), t))
        )
    own_q.wait()
    for copy in x_copies:
        copy.wait_recv()
    kv_copy.wait_recv()
    for copy in e_copies + m_copies + z_copies + x_copies + [kv_copy]:
        copy.wait_send()


def attend_kernel(meta_all, place, q_own, q_part, cache, kv_sib, o_own, l_own, o_part, l_part, kv, q, sems):
    r = place[0]
    t = place[1]
    par_dev, block = cache.shape[0], cache.shape[1]
    children, rows = o_own.shape[1], o_own.shape[2]
    loads = [
        pltpu.make_async_copy(cache, kv.at[pl.ds(0, par_dev)], sems.at[0]),
        pltpu.make_async_copy(kv_sib, kv.at[pl.ds(par_dev, par_dev)], sems.at[1]),
        pltpu.make_async_copy(q_own, q.at[0], sems.at[2]),
        pltpu.make_async_copy(q_part, q.at[1], sems.at[3]),
    ]
    for load in loads:
        load.start()
    for ref in (o_own, l_own, o_part, l_part):
        ref[...] = jnp.zeros(ref.shape, ref.dtype)
    for load in loads:
        load.wait()
    lane = lax.broadcasted_iota(jnp.int32, (rows, 128), 1)
    column = lax.broadcasted_iota(jnp.int32, (rows, block), 1) + t * block

    for side, (o_ref, l_ref) in enumerate(((o_own, l_own), (o_part, l_part))):

        def child(c, carry):
            parent = meta_all[2 * side, 4, c]
            owner = parent // par_dev
            local = lax.rem(parent, par_dev)
            away = jnp.where(owner == r, 0, 1)

            @pl.when(owner // 2 == r // 2)
            def _():
                length = meta_all[away, local, 0]
                slot = away * par_dev + local
                valid = column < length
                for k in range(KV_HEADS):
                    keys = kv[slot, :, k * HEAD : (k + 1) * HEAD]
                    values = kv[slot, :, (KV_HEADS + k) * HEAD : (KV_HEADS + k + 1) * HEAD]
                    scores = (
                        lax.dot_general(
                            q[side, k, c],
                            keys,
                            (((1,), (1,)), ((), ())),
                            preferred_element_type=jnp.float32,
                        )
                        * SCALE
                    )
                    scores = jnp.where(valid, scores, NEG)
                    top = jnp.max(scores, axis=-1, keepdims=True)
                    weights = jnp.where(valid, jnp.exp(scores - top), 0.0)
                    total = jnp.sum(weights, axis=-1, keepdims=True)
                    summed = jnp.dot(
                        weights.astype(jnp.bfloat16), values, preferred_element_type=jnp.float32
                    )
                    some = total > 0.0
                    safe = jnp.where(some, total, 1.0)
                    o_ref[k, c] = (summed / safe).astype(jnp.bfloat16)
                    lse = jnp.where(some, top + jnp.log(safe), NEG)
                    l_ref[k] = jnp.where(lane == c, lse, l_ref[k])

            return carry

        lax.fori_loop(0, children, child, 0)


def finish_kernel(
    o_own,
    l_own,
    o_part,
    l_part,
    o_self,
    l_self,
    wo,
    out,
    rx_o,
    rx_l,
    mo,
    ml,
    ao,
    al,
    att,
    abuf,
    wob,
    acc,
    xo_s,
    xo_r,
    xl_s,
    xl_r,
    zo_s,
    zo_r,
    zl_s,
    zl_r,
    a_s,
    a_r,
    w_s,
):
    part = lax.axis_index("parts")
    r = lax.axis_index("replica")
    t = lax.axis_index("tensor")
    children, rows = o_own.shape[1], o_own.shape[2]
    steps = rows // GROUP
    deep = GROUP * HEAD

    def at(rep, ten):
        return (part, rep, ten)

    loads = []
    for d in range(4):
        k = flip(t, d)
        loads.append(
            pltpu.make_async_copy(
                wo.at[pl.ds(pl.multiple_of(k * deep, deep), deep)], wob.at[d], w_s.at[d]
            )
        )
        loads[-1].start()
    greet([at(r, flip(t, d)) for d in (1, 2, 3)] + [at(flip(r, 2), t)])
    order = (3, 2, 1, 0)
    x_copies = {}
    for d in order:
        k = flip(t, d)
        x_copies[d] = (
            send(o_part.at[k], rx_o.at[d], (xo_s, xo_r), d, at(flip(r, 2), t)),
            send(l_part.at[k], rx_l.at[d], (xl_s, xl_r), d, at(flip(r, 2), t)),
        )
    z_copies = {}
    for d in order:
        k = flip(t, d)
        for copy in x_copies[d]:
            copy.wait_recv()
        mo[d] = o_own[k] + rx_o[d]
        ml[d] = l_own[k] + rx_l[d]
        if d:
            z_copies[d] = (
                send(mo.at[d], ao.at[d - 1], (zo_s, zo_r), d - 1, at(r, k)),
                send(ml.at[d], al.at[d - 1], (zl_s, zl_r), d - 1, at(r, k)),
            )
    for d in (1, 2, 3):
        for copy in z_copies[d]:
            copy.wait_recv()
    lses = [ml[0], l_self[...]] + [al[d] for d in range(3)]
    top = functools.reduce(jnp.maximum, lses)
    shares = [jnp.exp(lse - top) for lse in lses]
    inverse = 1.0 / functools.reduce(jnp.add, shares)
    shares = [share * inverse for share in shares]
    for c in range(0, children, 2):
        both = []
        for one in (c, c + 1):
            pieces = [mo[0, one], o_self[one]] + [ao[d, one] for d in range(3)]
            mixed = jnp.zeros((rows, HEAD), jnp.float32)
            for share, piece in zip(shares, pieces):
                mixed = mixed + share[:, one : one + 1] * piece.astype(jnp.float32)
            both.append(mixed)
        for g in range(GROUP):
            pair = jnp.concatenate([m[g * steps : (g + 1) * steps] for m in both], axis=0)
            att[c * steps : (c + 2) * steps, g * HEAD : (g + 1) * HEAD] = pair.astype(jnp.bfloat16)
    a_copies = [
        send(att, abuf.at[d - 1], (a_s, a_r), d - 1, at(r, flip(t, d))) for d in (1, 2, 3)
    ]
    for d in range(4):
        if d:
            a_copies[d - 1].wait_recv()
        block = att[...] if d == 0 else abuf[d - 1]
        loads[d].wait()
        more = jnp.dot(block, wob[d], preferred_element_type=jnp.float32)
        if d == 0:
            acc[...] = more
        elif d < 3:
            acc[...] += more
        else:
            out[...] = (acc[...] + more).astype(out.dtype)
    for copy in a_copies:
        copy.wait_send()
    for d in range(4):
        for copy in x_copies[d]:
            copy.wait_send()
        if d:
            for copy in z_copies[d]:
                copy.wait_send()


def at_parents(embedded, w_query, w_key, w_value, w_out, prefix_cache, prefix_len, child_parent):
    steps, children, width = embedded.shape
    rows = steps * children
    par_dev, block, kv_width = prefix_cache.shape
    tall = GROUP * steps
    out_width = w_out.shape[1]
    bf16, f32, i32 = jnp.bfloat16, jnp.float32, jnp.int32
    any_space = pl.BlockSpec(memory_space=pl.ANY)
    vmem = pl.BlockSpec(memory_space=pltpu.VMEM)
    smem = pl.BlockSpec(memory_space=pltpu.SMEM)
    dma = pltpu.SemaphoreType.DMA
    shape = jax.ShapeDtypeStruct

    emb = jnp.transpose(embedded, (1, 0, 2)).reshape(rows, width)
    lens = jnp.broadcast_to(prefix_len[:, None], (par_dev, 128))
    names = jnp.pad(child_parent[None, :], ((0, 0), (0, 128 - children)))
    meta = jnp.concatenate([lens, names, jnp.zeros((8 - par_dev - 1, 128), i32)], axis=0)
    cpb = jnp.broadcast_to(jnp.repeat(child_parent, steps)[:, None], (rows, 128))
    half = HEAD // 2
    freq = ROPE_BASE ** (-jnp.arange(half, dtype=f32) / half)
    freq = jnp.concatenate([freq, freq])[None, :]
    place = jnp.stack([lax.axis_index("replica"), lax.axis_index("tensor")]).astype(i32)

    q_own, q_part, kv_sib, meta_all, o_self, l_self = pl.pallas_call(
        project_kernel,
        out_shape=(
            shape((KV_HEADS, children, tall, HEAD), bf16),
            shape((KV_HEADS, children, tall, HEAD), bf16),
            shape(prefix_cache.shape, bf16),
            shape((4, 8, 128), i32),
            shape((children, tall, HEAD), f32),
            shape((tall, 128), f32),
        ),
        in_specs=[vmem, vmem, vmem, vmem, any_space, any_space, any_space, any_space],
        out_specs=(any_space, any_space, any_space, vmem, vmem, vmem),
        scratch_shapes=[
            pltpu.VMEM((3, rows, width), bf16),
            pltpu.VMEM((4, width, w_query.shape[1]), bf16),
            pltpu.VMEM((4, width, 2 * HEAD), bf16),
            pltpu.VMEM((rows, w_query.shape[1]), f32),
            pltpu.VMEM((rows, 2 * HEAD), f32),
            pltpu.VMEM((children, tall, HEAD), bf16),
            dma((3,)),
            dma((3,)),
            dma((12,)),
            dma((3,)),
            dma((3,)),
            dma((4,)),
            dma((4,)),
            dma((3,)),
            dma((3,)),
            dma((1,)),
            dma((1,)),
            dma((2,)),
        ],
        compiler_params=pltpu.CompilerParams(
            collective_id=0, has_side_effects=True, vmem_limit_bytes=40 * 2**20
        ),
        name="project",
    )(emb, meta, cpb, freq, w_query, w_key, w_value, prefix_cache)

    values_shape = shape((KV_HEADS, children, tall, HEAD), bf16)
    lse_shape = shape((KV_HEADS, tall, 128), f32)
    o_own, l_own, o_part, l_part = pl.pallas_call(
        attend_kernel,
        out_shape=(values_shape, lse_shape, values_shape, lse_shape),
        in_specs=[smem, smem, any_space, any_space, any_space, any_space],
        out_specs=(vmem, vmem, vmem, vmem),
        scratch_shapes=[
            pltpu.VMEM((2 * par_dev, block, kv_width), bf16),
            pltpu.VMEM((2, KV_HEADS, children, tall, HEAD), bf16),
            dma((4,)),
        ],
        compiler_params=pltpu.CompilerParams(vmem_limit_bytes=40 * 2**20),
        name="attend",
    )(meta_all, place, q_own, q_part, prefix_cache, kv_sib)

    result = pl.pallas_call(
        finish_kernel,
        out_shape=shape((rows, out_width), bf16),
        in_specs=[vmem] * 6 + [any_space],
        out_specs=vmem,
        scratch_shapes=[
            pltpu.VMEM((4, children, tall, HEAD), bf16),
            pltpu.VMEM((4, tall, 128), f32),
            pltpu.VMEM((4, children, tall, HEAD), bf16),
            pltpu.VMEM((4, tall, 128), f32),
            pltpu.VMEM((3, children, tall, HEAD), bf16),
            pltpu.VMEM((3, tall, 128), f32),
            pltpu.VMEM((rows, GROUP * HEAD), bf16),
            pltpu.VMEM((3, rows, GROUP * HEAD), bf16),
            pltpu.VMEM((4, GROUP * HEAD, out_width), bf16),
            pltpu.VMEM((rows, out_width), f32),
            dma((4,)),
            dma((4,)),
            dma((4,)),
            dma((4,)),
            dma((3,)),
            dma((3,)),
            dma((3,)),
            dma((3,)),
            dma((3,)),
            dma((3,)),
            dma((4,)),
        ],
        compiler_params=pltpu.CompilerParams(
            collective_id=1, has_side_effects=True, vmem_limit_bytes=40 * 2**20
        ),
        name="finish",
    )(o_own, l_own, o_part, l_part, o_self, l_self, w_out)
    return jnp.transpose(result.reshape(children, steps, out_width), (1, 0, 2))


def solution(mesh):
    in_specs = (
        P(None, ("parts", "replica"), "tensor"),
        P(None, "tensor"),
        P(None, "tensor"),
        P(None, "tensor"),
        P(None, "tensor"),
        P(("parts", "replica"), "tensor", None),
        P(("parts", "replica")),
        P(("parts", "replica")),
    )
    out_specs = P(None, ("parts", "replica"), "tensor")
    fits = mesh.shape["replica"] == 4 and mesh.shape["tensor"] == KV_HEADS
    body = at_parents if fits else per_device
    return jax.shard_map(
        body, mesh=mesh, in_specs=in_specs, out_specs=out_specs, check_vma=False
    )
```

```python
import functools

import jax
import jax.numpy as jnp
from jax import lax
from jax.experimental import pallas as pl
from jax.experimental.pallas import tpu as pltpu
from jax.sharding import PartitionSpec as P

HEADS = 32
KV_HEADS = 4
HEAD = 128


EPS = 1e-06
NEG = -1e30
ROPE_BASE = 1000000.0


def combined_all(x, axis, combine):
    everything = jax.tree.map(
        lambda part, kind: lax.all_gather(part.astype(kind), axis),
        x,
        (jnp.bfloat16, jnp.bfloat16, jnp.bfloat16),
    )

    def take(k):
        return jax.tree.map(lambda part, own: part[k].astype(own.dtype), everything, x)

    return lax.fori_loop(
        1, lax.axis_size(axis), lambda k, so_far: combine(so_far, take(k)), take(0)
    )


def rotate(values, positions):
    half = values.shape[-1] // 2
    freq = ROPE_BASE ** (-jnp.arange(half, dtype=jnp.float32) / half)
    angle = positions.astype(jnp.float32)[..., None] * freq
    cosine = jnp.cos(angle)
    sine = jnp.sin(angle)
    first = values[..., :half]
    second = values[..., half:]
    return jnp.concatenate(
        [first * cosine - second * sine, first * sine + second * cosine], axis=-1
    )


def combine(first, second):
    upper = jnp.maximum(first[0], second[0])
    left = jnp.exp(first[0] - upper)
    right = jnp.exp(second[0] - upper)
    return (
        upper,
        first[1] * left + second[1] * right,
        first[2] * left[..., None] + second[2] * right[..., None],
    )


def rms_normed(current):
    whole = current.astype(jnp.float32)
    return (whole * lax.rsqrt(jnp.mean(whole * whole, axis=-1, keepdims=True) + EPS)).astype(
        jnp.bfloat16
    )


def per_device(embedded, w_query, w_key, w_value, w_out, prefix_cache, prefix_len, child_parent):
    steps = embedded.shape[0]
    rows = embedded.shape[1]
    par_dev, pos_dev, width = prefix_cache.shape
    kv_width = width // 2
    group = HEADS // KV_HEADS
    scale = HEAD ** (-0.5)
    table = lax.all_gather(prefix_cache, "replica", axis=0, tiled=True)
    lengths_all = lax.all_gather(prefix_len, "replica", axis=0, tiled=True)
    lengths = lengths_all[child_parent]
    chosen = jnp.take(table, child_parent, axis=0)
    keys = jnp.transpose(
        chosen[:, :, :kv_width].reshape(rows, pos_dev, KV_HEADS, HEAD), (0, 2, 1, 3)
    )
    values = jnp.transpose(
        chosen[:, :, kv_width:].reshape(rows, pos_dev, KV_HEADS, HEAD), (0, 2, 1, 3)
    )
    positions = lax.axis_index("tensor") * pos_dev + jnp.arange(pos_dev, dtype=jnp.int32)
    valid = positions[None, :] < lengths[:, None]
    block_mask = valid[:, None, None, :]
    features = jnp.stack(
        [lax.all_gather(embedded[step], "tensor", axis=1, tiled=True) for step in range(steps)],
        axis=0,
    )
    normed = rms_normed(features).reshape(steps * rows, -1)
    position = lengths[None, :] + jnp.arange(steps, dtype=jnp.int32)[:, None]
    query_part = jnp.dot(normed, w_query, preferred_element_type=jnp.float32)
    local_heads = query_part.shape[1] // HEAD
    query_part = (
        rotate(query_part.reshape(steps, rows, local_heads, HEAD), position[:, :, None])
        .reshape(steps, rows, local_heads * HEAD)
        .astype(jnp.bfloat16)
    )
    key_part = (
        jnp.dot(normed, w_key, preferred_element_type=jnp.float32)
        .astype(jnp.bfloat16)
        .reshape(steps, rows, -1)
    )
    value_part = (
        jnp.dot(normed, w_value, preferred_element_type=jnp.float32)
        .astype(jnp.bfloat16)
        .reshape(steps, rows, -1)
    )
    query_all, key_all, value_all = (
        lax.all_gather(query_part, "tensor", axis=2, tiled=True),
        lax.all_gather(key_part, "tensor", axis=2, tiled=True),
        lax.all_gather(value_part, "tensor", axis=2, tiled=True),
    )
    own_keys = rotate(
        key_all.astype(jnp.float32).reshape(steps, rows, KV_HEADS, HEAD), position[:, :, None]
    ).astype(jnp.bfloat16)
    own_values = value_all.reshape(steps, rows, KV_HEADS, HEAD)
    queries = query_all.reshape(steps, rows, KV_HEADS, group, HEAD)
    scores = (
        jnp.einsum("sckgd,ckpd->sckgp", queries, keys, preferred_element_type=jnp.float32) * scale
    )
    full_mask = block_mask[None]
    scores = jnp.where(full_mask, scores, NEG)
    upper = jnp.max(scores, axis=-1)
    weights = jnp.where(full_mask, jnp.exp(scores - upper[..., None]), 0.0)
    total = jnp.sum(weights, axis=-1)
    partial_value = jnp.einsum(
        "sckgp,ckpd->sckgd",
        weights.astype(jnp.bfloat16),
        values,
        preferred_element_type=jnp.float32,
    )
    merged = combined_all((upper, total, partial_value), "tensor", combine)
    causal = (jnp.arange(steps)[None, :] <= jnp.arange(steps)[:, None])[:, None, None, None, :]
    own_scores = (
        jnp.einsum("sckgd,tckd->sckgt", queries, own_keys, preferred_element_type=jnp.float32)
        * scale
    )
    own_scores = jnp.where(causal, own_scores, NEG)
    own_upper = jnp.max(own_scores, axis=-1)
    own_weights = jnp.where(causal, jnp.exp(own_scores - own_upper[..., None]), 0.0)
    own_total = jnp.sum(own_weights, axis=-1)
    own_partial = jnp.einsum(
        "sckgt,tckd->sckgd",
        own_weights.astype(jnp.bfloat16),
        own_values,
        preferred_element_type=jnp.float32,
    )
    final = combine(merged, (own_upper, own_total, own_partial))
    attended = (
        (final[2] / final[1][..., None]).reshape(steps * rows, HEADS * HEAD).astype(jnp.bfloat16)
    )
    result = jnp.dot(attended, w_out, preferred_element_type=jnp.float32).astype(jnp.bfloat16)
    return result.reshape(steps, rows, -1)


GROUP = HEADS // KV_HEADS
SCALE = HEAD ** (-0.5)
LOG2E = 1.4426950408889634
UNROLL = 4
MESH = pl.DeviceIdType.MESH


def flip(index, step):
    if step == 0:
        return index
    if step == 1:
        return index + 1 - 2 * lax.rem(index, 2)
    if step == 2:
        return index + 2 - 4 * (index // 2)
    return 3 - index


def send(src, dst, sems, slot, device):
    copy = pltpu.make_async_remote_copy(
        src_ref=src,
        dst_ref=dst,
        send_sem=sems[0].at[slot],
        recv_sem=sems[1].at[slot],
        device_id=device,
        device_id_type=MESH,
    )
    copy.start()
    return copy


def greet(devices):
    barrier = pltpu.get_barrier_semaphore()
    for device in devices:
        pl.semaphore_signal(barrier, inc=1, device_id=device, device_id_type=MESH)
    pl.semaphore_wait(barrier, len(devices))


def compact(column, children, rows):
    lane = lax.broadcasted_iota(jnp.int32, (rows, 128), 1)
    out = jnp.zeros((rows, 128), jnp.float32)
    for c in range(children):
        out = jnp.where(lane == c, column[c * rows : (c + 1) * rows], out)
    return out


def forked_kernel(
    lens,
    names,
    emb,
    freq,
    wq,
    wk,
    wv,
    wo,
    cache,
    out,
    meta,
    metas,
    meta_s,
    ebuf,
    wqb,
    wkb,
    wob,
    accq,
    acck,
    kv,
    q_own,
    q_part,
    o_own,
    o_part,
    l_part,
    o_self,
    rx_o,
    rx_l,
    mo,
    ml,
    ao,
    al,
    att,
    abuf,
    acc,
    e_s,
    e_r,
    w_s,
    wo_s,
    q_s,
    q_r,
    x_s,
    x_r,
    m_s,
    m_r,
    k_s,
    k_r,
    loc_s,
    xo_s,
    xo_r,
    xl_s,
    xl_r,
    zo_s,
    zo_r,
    zl_s,
    zl_r,
    a_s,
    a_r,
):
    part = lax.axis_index("parts")
    r = lax.axis_index("replica")
    t = lax.axis_index("tensor")
    rows, width = emb.shape
    children, tall = q_own.shape[1], q_own.shape[2]
    steps = rows // children
    par_dev, block = cache.shape[0], cache.shape[1]
    deep = GROUP * HEAD

    def at(rep, ten):
        return (part, rep, ten)

    def local(src, dst, sem):
        copy = pltpu.make_async_copy(src, dst, sem)
        copy.start()
        return copy

    lane = lax.broadcasted_iota(jnp.int32, (8, 128), 1)
    table = jnp.zeros((8, 128), jnp.int32)
    for i in range(par_dev):
        table = jnp.where(lane == i, lens[i], table)
    for c in range(children):
        table = jnp.where(lane == 16 + c, names[c], table)
    meta[...] = table

    loads = []
    for d in range(4):
        k = flip(t, d)
        span = pl.ds(pl.multiple_of(k * width, width), width)
        loads.append(
            (
                local(wq.at[span], wqb.at[d], w_s.at[3 * d]),
                local(wk.at[span], wkb.at[d, :, pl.ds(0, HEAD)], w_s.at[3 * d + 1]),
                local(wv.at[span], wkb.at[d, :, pl.ds(HEAD, HEAD)], w_s.at[3 * d + 2]),
            )
        )

    greet([at(r, flip(t, d)) for d in (1, 2, 3)] + [at(flip(r, d), t) for d in (1, 2, 3)])
    m_copies = [
        send(meta, metas.at[d], (m_s, m_r), d - 1, at(flip(r, d), t)) for d in (1, 2, 3)
    ]
    e_copies = [
        send(emb, ebuf.at[d - 1], (e_s, e_r), d - 1, at(r, flip(t, d))) for d in (3, 2, 1)
    ][::-1]
    kv_copy = send(
        cache, kv.at[pl.ds(par_dev, par_dev)], (k_s, k_r), 0, at(flip(r, 1), t)
    )
    kv_own = local(cache, kv.at[pl.ds(0, par_dev)], loc_s.at[0])
    metas[0] = table
    for copy in m_copies:
        copy.wait_recv()
    meta_copy = local(metas, meta_s, loc_s.at[1])
    out_loads = []
    for d in range(4):
        k = flip(t, d)
        out_loads.append(
            local(wo.at[pl.ds(pl.multiple_of(k * deep, deep), deep)], wob.at[d], wo_s.at[d])
        )
    meta_copy.wait()

    def parent_of(side, c):
        name = meta_s[2 * side, 0, 16 + c]
        owner = lax.div(name, par_dev)
        which = lax.rem(name, par_dev)
        away = jnp.where(lax.rem(owner, 2) == lax.rem(r, 2), 0, 1)
        other = jnp.where(lax.div(owner, 2) == lax.div(r, 2), 0, 1)
        return other == 0, away * par_dev + which, meta_s[2 * other + away, 0, which]

    step = lax.broadcasted_iota(jnp.int32, (steps, 128), 0)
    position = jnp.concatenate([parent_of(0, c)[2] + step for c in range(children)], axis=0)
    angle = position.astype(jnp.float32) * freq[...]
    cosine = jnp.cos(angle)
    half = lax.broadcasted_iota(jnp.int32, (rows, 128), 1) < HEAD // 2
    sine = jnp.sin(angle)
    sine = jnp.where(half, -sine, sine)

    squares = jnp.zeros((rows, 1), jnp.float32)
    for d in range(4):
        if d:
            e_copies[d - 1].wait_recv()
        block_in = emb[...] if d == 0 else ebuf[d - 1]
        whole = block_in.astype(jnp.float32)
        squares = squares + jnp.sum(whole * whole, axis=-1, keepdims=True)
        for load in loads[d]:
            load.wait()
        more_q = jnp.dot(block_in, wqb[d], preferred_element_type=jnp.float32)
        more_k = jnp.dot(block_in, wkb[d], preferred_element_type=jnp.float32)
        if d == 0:
            accq[...] = more_q
            acck[...] = more_k
        else:
            accq[...] += more_q
            acck[...] += more_k
    norm = lax.rsqrt(squares / (4 * width) + EPS)

    def turn(x):
        return x * cosine + pltpu.roll(x, HEAD // 2, 1) * sine

    def head_of(g):
        x = turn(accq[:, g * HEAD : (g + 1) * HEAD] * norm)
        return x.reshape(children, steps, HEAD)

    for j in range(GROUP // 2):
        pair = jnp.concatenate([head_of(2 * j), head_of(2 * j + 1)], axis=1)
        q_own[0, :, 2 * steps * j : 2 * steps * (j + 1), :] = pair.astype(jnp.bfloat16)

    partner = at(flip(r, 2), t)
    x_copies = [send(q_own.at[0], q_part.at[0], (x_s, x_r), 0, partner)]
    z_copies = [
        send(q_own.at[0], q_own.at[d], (q_s, q_r), d - 1, at(r, flip(t, d))) for d in (1, 2, 3)
    ]

    key_raw = (acck[:, :HEAD] * norm).astype(jnp.bfloat16).astype(jnp.float32)
    key_new = turn(key_raw).astype(jnp.bfloat16)
    value = (acck[:, HEAD:] * norm).astype(jnp.bfloat16)
    total_rows = children * tall
    scores = (
        lax.dot_general(
            q_own[0].reshape(total_rows, HEAD),
            key_new,
            (((1,), (1,)), ((), ())),
            preferred_element_type=jnp.float32,
        )
        * SCALE
    )
    row = lax.broadcasted_iota(jnp.int32, (total_rows, rows), 0)
    col = lax.broadcasted_iota(jnp.int32, (total_rows, rows), 1)
    valid = (row // tall == col // steps) & (lax.rem(col, steps) <= lax.rem(row, steps))
    scores = jnp.where(valid, scores, NEG)
    top = jnp.max(scores, axis=-1, keepdims=True)
    weights = jnp.where(valid, jnp.exp(scores - top), 0.0)
    total = jnp.sum(weights, axis=-1, keepdims=True)
    summed = jnp.dot(weights.astype(jnp.bfloat16), value, preferred_element_type=jnp.float32)
    o_self[...] = (summed / total).reshape(children, tall, HEAD)
    l_self = compact(top + jnp.log(total), children, tall)

    kv_own.wait()
    kv_copy.wait_recv()
    column = lax.broadcasted_iota(jnp.int32, (tall, block), 1) + t * block
    lanes = lax.broadcasted_iota(jnp.int32, (tall, 128), 1)

    def attend(side, q, o_ref, head):
        first = pl.multiple_of(head * HEAD, HEAD)
        second = pl.multiple_of((KV_HEADS + head) * HEAD, HEAD)

        def some(i, lses):
            for u in range(UNROLL):
                c = i * UNROLL + u
                here, slot, length = parent_of(side, c)
                seen = jnp.logical_and(here, length > t * block)
                raw = lax.dot_general(
                    q[c],
                    kv[slot, :, pl.ds(first, HEAD)],
                    (((1,), (1,)), ((), ())),
                    preferred_element_type=jnp.float32,
                )
                raw = jnp.where(column < length, raw, NEG)
                peak = jnp.max(raw, axis=-1, keepdims=True)
                portion = jnp.exp2((raw - peak) * (SCALE * LOG2E))
                sums = jnp.sum(portion, axis=-1, keepdims=True)
                mixed = jnp.dot(
                    portion.astype(jnp.bfloat16),
                    kv[slot, :, pl.ds(second, HEAD)],
                    preferred_element_type=jnp.float32,
                )
                o_ref[c] = jnp.where(seen, mixed / sums, 0.0).astype(jnp.bfloat16)
                lse = jnp.where(seen, peak * SCALE + jnp.log(sums), NEG)
                lse = jnp.where(here, lse, 0.0)
                lses = jnp.where(lanes == c, lse, lses)
            return lses

        return lax.fori_loop(0, children // UNROLL, some, jnp.zeros((tall, 128), jnp.float32))

    r_copies = []
    t_copies = []

    def merge(d):
        for copy in r_copies[d]:
            copy.wait_recv()
        mo[d] = o_own[d] + rx_o[d]
        ml[d] = ml[d] + rx_l[d]
        if d:
            t_copies.append(
                (
                    send(mo.at[d], ao.at[d - 1], (zo_s, zo_r), d - 1, at(r, flip(t, d))),
                    send(ml.at[d], al.at[d - 1], (zl_s, zl_r), d - 1, at(r, flip(t, d))),
                )
            )

    def forward(d):
        z_copies[d - 1].wait_recv()
        x_copies.append(send(q_own.at[d], q_part.at[d], (x_s, x_r), d, partner))

    for d in range(4):
        head = flip(t, d)
        ml[d] = attend(0, q_own.at[d], o_own.at[d], head)
        if d < 3:
            forward(d + 1)
        x_copies[d].wait_recv()
        l_part[d] = attend(1, q_part.at[d], o_part.at[d], head)
        r_copies.append(
            (
                send(o_part.at[d], rx_o.at[d], (xo_s, xo_r), d, partner),
                send(l_part.at[d], rx_l.at[d], (xl_s, xl_r), d, partner),
            )
        )
        if d:
            merge(d - 1)
    merge(3)

    for copies in t_copies:
        for copy in copies:
            copy.wait_recv()
    lses = [ml[0], l_self] + [al[d] for d in range(3)]
    top = functools.reduce(jnp.maximum, lses)
    shares = [jnp.exp(lse - top) for lse in lses]
    inverse = 1.0 / functools.reduce(jnp.add, shares)
    shares = [share * inverse for share in shares]
    for c in range(0, children, 2):
        both = []
        for one in (c, c + 1):
            pieces = [mo[0, one], o_self[one]] + [ao[d, one] for d in range(3)]
            blend = jnp.zeros((tall, HEAD), jnp.float32)
            for share, piece in zip(shares, pieces):
                blend = blend + share[:, one : one + 1] * piece.astype(jnp.float32)
            both.append(blend)
        for g in range(GROUP):
            pair = jnp.concatenate([m[g * steps : (g + 1) * steps] for m in both], axis=0)
            att[c * steps : (c + 2) * steps, g * HEAD : (g + 1) * HEAD] = pair.astype(jnp.bfloat16)
    a_copies = [
        send(att, abuf.at[d - 1], (a_s, a_r), d - 1, at(r, flip(t, d))) for d in (3, 2, 1)
    ][::-1]
    for d in range(4):
        if d:
            a_copies[d - 1].wait_recv()
        block_in = att[...] if d == 0 else abuf[d - 1]
        out_loads[d].wait()
        more = jnp.dot(block_in, wob[d], preferred_element_type=jnp.float32)
        if d == 0:
            acc[...] = more
        elif d < 3:
            acc[...] += more
        else:
            out[...] = (acc[...] + more).astype(out.dtype)
    for copies in r_copies + t_copies:
        for copy in copies:
            copy.wait_send()
    for copy in e_copies + m_copies + z_copies + x_copies + a_copies + [kv_copy]:
        copy.wait_send()


def at_parents(embedded, w_query, w_key, w_value, w_out, prefix_cache, prefix_len, child_parent):
    steps, children, width = embedded.shape
    rows = steps * children
    par_dev, block, kv_width = prefix_cache.shape
    tall = GROUP * steps
    out_width = w_out.shape[1]
    bf16, f32, i32 = jnp.bfloat16, jnp.float32, jnp.int32
    any_space = pl.BlockSpec(memory_space=pl.ANY)
    vmem = pl.BlockSpec(memory_space=pltpu.VMEM)
    smem = pl.BlockSpec(memory_space=pltpu.SMEM)

    emb = jnp.transpose(embedded, (1, 0, 2)).reshape(rows, width)
    half = HEAD // 2
    freq = ROPE_BASE ** (-jnp.arange(half, dtype=f32) / half)
    freq = jnp.concatenate([freq, freq])[None, :]

    def scratch(shape, kind=bf16):
        return pltpu.VMEM(shape, kind)

    result = pl.pallas_call(
        forked_kernel,
        out_shape=jax.ShapeDtypeStruct((rows, out_width), bf16),
        in_specs=[smem, smem, vmem, vmem] + [any_space] * 5,
        out_specs=vmem,
        scratch_shapes=[
            scratch((8, 128), i32),
            scratch((4, 8, 128), i32),
            pltpu.SMEM((4, 8, 128), i32),
            scratch((3, rows, width)),
            scratch((4, width, w_query.shape[1])),
            scratch((4, width, 2 * HEAD)),
            scratch((4, GROUP * HEAD, out_width)),
            scratch((rows, w_query.shape[1]), f32),
            scratch((rows, 2 * HEAD), f32),
            scratch((2 * par_dev, block, kv_width)),
            scratch((4, children, tall, HEAD)),
            scratch((4, children, tall, HEAD)),
            scratch((4, children, tall, HEAD)),
            scratch((4, children, tall, HEAD)),
            scratch((4, tall, 128), f32),
            scratch((children, tall, HEAD), f32),
            scratch((4, children, tall, HEAD)),
            scratch((4, tall, 128), f32),
            scratch((4, children, tall, HEAD)),
            scratch((4, tall, 128), f32),
            scratch((3, children, tall, HEAD)),
            scratch((3, tall, 128), f32),
            scratch((rows, GROUP * HEAD)),
            scratch((3, rows, GROUP * HEAD)),
            scratch((rows, out_width), f32),
        ]
        + [
            pltpu.SemaphoreType.DMA((n,))
            for n in (3, 3, 12, 4, 3, 3, 4, 4, 3, 3, 1, 1, 2, 4, 4, 4, 4, 3, 3, 3, 3, 3, 3)
        ],
        compiler_params=pltpu.CompilerParams(
            collective_id=0, has_side_effects=True, vmem_limit_bytes=60 * 2**20
        ),
        name="forked",
    )(prefix_len, child_parent, emb, freq, w_query, w_key, w_value, w_out, prefix_cache)
    return jnp.transpose(result.reshape(children, steps, out_width), (1, 0, 2))


def solution(mesh):
    in_specs = (
        P(None, ("parts", "replica"), "tensor"),
        P(None, "tensor"),
        P(None, "tensor"),
        P(None, "tensor"),
        P(None, "tensor"),
        P(("parts", "replica"), "tensor", None),
        P(("parts", "replica")),
        P(("parts", "replica")),
    )
    out_specs = P(None, ("parts", "replica"), "tensor")
    fits = mesh.shape["replica"] == 4 and mesh.shape["tensor"] == KV_HEADS
    body = at_parents if fits else per_device
    return jax.shard_map(
        body, mesh=mesh, in_specs=in_specs, out_specs=out_specs, check_vma=False
    )
```

```python
import functools

import jax
import jax.numpy as jnp
import numpy as np
from jax import lax
from jax.experimental import pallas as pl
from jax.experimental.pallas import tpu as pltpu
from jax.sharding import PartitionSpec as P

HEADS = 32
KV_HEADS = 4
HEAD = 128


EPS = 1e-06
NEG = -1e30
ROPE_BASE = 1000000.0


def combined_all(x, axis, combine):
    everything = jax.tree.map(
        lambda part, kind: lax.all_gather(part.astype(kind), axis),
        x,
        (jnp.bfloat16, jnp.bfloat16, jnp.bfloat16),
    )

    def take(k):
        return jax.tree.map(lambda part, own: part[k].astype(own.dtype), everything, x)

    return lax.fori_loop(
        1, lax.axis_size(axis), lambda k, so_far: combine(so_far, take(k)), take(0)
    )


def rotate(values, positions):
    half = values.shape[-1] // 2
    freq = ROPE_BASE ** (-jnp.arange(half, dtype=jnp.float32) / half)
    angle = positions.astype(jnp.float32)[..., None] * freq
    cosine = jnp.cos(angle)
    sine = jnp.sin(angle)
    first = values[..., :half]
    second = values[..., half:]
    return jnp.concatenate(
        [first * cosine - second * sine, first * sine + second * cosine], axis=-1
    )


def combine(first, second):
    upper = jnp.maximum(first[0], second[0])
    left = jnp.exp(first[0] - upper)
    right = jnp.exp(second[0] - upper)
    return (
        upper,
        first[1] * left + second[1] * right,
        first[2] * left[..., None] + second[2] * right[..., None],
    )


def rms_normed(current):
    whole = current.astype(jnp.float32)
    return (whole * lax.rsqrt(jnp.mean(whole * whole, axis=-1, keepdims=True) + EPS)).astype(
        jnp.bfloat16
    )


def per_device(embedded, w_query, w_key, w_value, w_out, prefix_cache, prefix_len, child_parent):
    steps = embedded.shape[0]
    rows = embedded.shape[1]
    par_dev, pos_dev, width = prefix_cache.shape
    kv_width = width // 2
    group = HEADS // KV_HEADS
    scale = HEAD ** (-0.5)
    table = lax.all_gather(prefix_cache, "replica", axis=0, tiled=True)
    lengths_all = lax.all_gather(prefix_len, "replica", axis=0, tiled=True)
    lengths = lengths_all[child_parent]
    chosen = jnp.take(table, child_parent, axis=0)
    keys = jnp.transpose(
        chosen[:, :, :kv_width].reshape(rows, pos_dev, KV_HEADS, HEAD), (0, 2, 1, 3)
    )
    values = jnp.transpose(
        chosen[:, :, kv_width:].reshape(rows, pos_dev, KV_HEADS, HEAD), (0, 2, 1, 3)
    )
    positions = lax.axis_index("tensor") * pos_dev + jnp.arange(pos_dev, dtype=jnp.int32)
    valid = positions[None, :] < lengths[:, None]
    block_mask = valid[:, None, None, :]
    features = jnp.stack(
        [lax.all_gather(embedded[step], "tensor", axis=1, tiled=True) for step in range(steps)],
        axis=0,
    )
    normed = rms_normed(features).reshape(steps * rows, -1)
    position = lengths[None, :] + jnp.arange(steps, dtype=jnp.int32)[:, None]
    query_part = jnp.dot(normed, w_query, preferred_element_type=jnp.float32)
    local_heads = query_part.shape[1] // HEAD
    query_part = (
        rotate(query_part.reshape(steps, rows, local_heads, HEAD), position[:, :, None])
        .reshape(steps, rows, local_heads * HEAD)
        .astype(jnp.bfloat16)
    )
    key_part = (
        jnp.dot(normed, w_key, preferred_element_type=jnp.float32)
        .astype(jnp.bfloat16)
        .reshape(steps, rows, -1)
    )
    value_part = (
        jnp.dot(normed, w_value, preferred_element_type=jnp.float32)
        .astype(jnp.bfloat16)
        .reshape(steps, rows, -1)
    )
    query_all, key_all, value_all = (
        lax.all_gather(query_part, "tensor", axis=2, tiled=True),
        lax.all_gather(key_part, "tensor", axis=2, tiled=True),
        lax.all_gather(value_part, "tensor", axis=2, tiled=True),
    )
    own_keys = rotate(
        key_all.astype(jnp.float32).reshape(steps, rows, KV_HEADS, HEAD), position[:, :, None]
    ).astype(jnp.bfloat16)
    own_values = value_all.reshape(steps, rows, KV_HEADS, HEAD)
    queries = query_all.reshape(steps, rows, KV_HEADS, group, HEAD)
    scores = (
        jnp.einsum("sckgd,ckpd->sckgp", queries, keys, preferred_element_type=jnp.float32) * scale
    )
    full_mask = block_mask[None]
    scores = jnp.where(full_mask, scores, NEG)
    upper = jnp.max(scores, axis=-1)
    weights = jnp.where(full_mask, jnp.exp(scores - upper[..., None]), 0.0)
    total = jnp.sum(weights, axis=-1)
    partial_value = jnp.einsum(
        "sckgp,ckpd->sckgd",
        weights.astype(jnp.bfloat16),
        values,
        preferred_element_type=jnp.float32,
    )
    merged = combined_all((upper, total, partial_value), "tensor", combine)
    causal = (jnp.arange(steps)[None, :] <= jnp.arange(steps)[:, None])[:, None, None, None, :]
    own_scores = (
        jnp.einsum("sckgd,tckd->sckgt", queries, own_keys, preferred_element_type=jnp.float32)
        * scale
    )
    own_scores = jnp.where(causal, own_scores, NEG)
    own_upper = jnp.max(own_scores, axis=-1)
    own_weights = jnp.where(causal, jnp.exp(own_scores - own_upper[..., None]), 0.0)
    own_total = jnp.sum(own_weights, axis=-1)
    own_partial = jnp.einsum(
        "sckgt,tckd->sckgd",
        own_weights.astype(jnp.bfloat16),
        own_values,
        preferred_element_type=jnp.float32,
    )
    final = combine(merged, (own_upper, own_total, own_partial))
    attended = (
        (final[2] / final[1][..., None]).reshape(steps * rows, HEADS * HEAD).astype(jnp.bfloat16)
    )
    result = jnp.dot(attended, w_out, preferred_element_type=jnp.float32).astype(jnp.bfloat16)
    return result.reshape(steps, rows, -1)


GROUP = HEADS // KV_HEADS
SCALE = HEAD ** (-0.5)
LOG2E = 1.4426950408889634
UNROLL = 4
MESH = pl.DeviceIdType.MESH


def flip(index, step):
    if step == 0:
        return index
    if step == 1:
        return index + 1 - 2 * lax.rem(index, 2)
    if step == 2:
        return index + 2 - 4 * (index // 2)
    return 3 - index


def remote(src, dst, sems, slot, device, landing=None):
    return pltpu.make_async_remote_copy(
        src_ref=src,
        dst_ref=dst,
        send_sem=sems[0].at[slot],
        recv_sem=sems[1].at[slot if landing is None else landing],
        device_id=device,
        device_id_type=MESH,
    )


def send(*args):
    copy = remote(*args)
    copy.start()
    return copy


def nth(t, i):
    return (t, flip(t, 1), 2 - t // 2, 3 - 3 * (t // 2))[i]


class LineGather:
    def __init__(self, own, slots, sems, at, r, t):
        self.middle = lax.rem((t + 1) // 2, 2) == 1
        end, other = at(r, flip(t, 1)), at(r, 3 - t)
        plan = (
            (own, 1, end),
            (own, 2, other),
            (slots(1), 3, other),
            (slots(2), 2, end),
            (slots(3), 3, end),
        )
        self.copies = [
            remote(src, slots(to), sems, n, device, to - 1)
            for n, (src, to, device) in enumerate(plan)
        ]
        self.landings = [remote(slots(i), slots(i), sems, 0, end, i - 1) for i in (1, 2, 3)]
        self.copies[0].start()
        self.if_middle(self.copies[1].start)

    def if_middle(self, act):
        @pl.when(self.middle)
        def _():
            act()

    def arrived(self, i):
        self.landings[i - 1].wait_recv()
        self.if_middle(self.copies[i + 1].start)

    def finish(self):
        self.copies[0].wait_send()

        @pl.when(self.middle)
        def _():
            for copy in self.copies[1:]:
                copy.wait_send()


def greet(devices):
    barrier = pltpu.get_barrier_semaphore()
    for device in devices:
        pl.semaphore_signal(barrier, inc=1, device_id=device, device_id_type=MESH)
    pl.semaphore_wait(barrier, len(devices))


def compact(column, children, rows):
    lane = lax.broadcasted_iota(jnp.int32, (rows, 128), 1)
    out = jnp.zeros((rows, 128), jnp.float32)
    for c in range(children):
        out = jnp.where(lane == c, column[c * rows : (c + 1) * rows], out)
    return out


def forked_kernel(
    lens,
    names,
    emb,
    freq,
    wq,
    wk,
    wv,
    wo,
    cache,
    out,
    meta,
    metas,
    meta_s,
    ebuf,
    wqb,
    wkb,
    wob,
    accq,
    acck,
    heads,
    kv,
    q_own,
    q_part,
    o_own,
    o_part,
    l_part,
    o_self,
    rx_o,
    rx_l,
    mo,
    ml,
    ao,
    al,
    att,
    abuf,
    acc,
    e_s,
    e_r,
    w_s,
    wo_s,
    q_s,
    q_r,
    x_s,
    x_r,
    m_s,
    m_r,
    k_s,
    k_r,
    loc_s,
    xo_s,
    xo_r,
    xl_s,
    xl_r,
    zo_s,
    zo_r,
    zl_s,
    zl_r,
    a_s,
    a_r,
):
    part = lax.axis_index("parts")
    r = lax.axis_index("replica")
    t = lax.axis_index("tensor")
    rows, width = emb.shape
    children, tall = q_own.shape[1], q_own.shape[2]
    steps = rows // children
    par_dev, block = cache.shape[0], cache.shape[1]
    deep = GROUP * HEAD

    def at(rep, ten):
        return (part, rep, ten)

    def local(src, dst, sem):
        copy = pltpu.make_async_copy(src, dst, sem)
        copy.start()
        return copy

    lane = lax.broadcasted_iota(jnp.int32, (8, 128), 1)
    table = jnp.zeros((8, 128), jnp.int32)
    for i in range(par_dev):
        table = jnp.where(lane == i, lens[i], table)
    for c in range(children):
        table = jnp.where(lane == 16 + c, names[c], table)
    meta[...] = table

    loads = []
    for d in range(4):
        k = nth(t, d)
        span = pl.ds(pl.multiple_of(k * width, width), width)
        loads.append(
            (
                local(wq.at[span], wqb.at[d], w_s.at[3 * d]),
                local(wk.at[span], wkb.at[d, :, pl.ds(0, HEAD)], w_s.at[3 * d + 1]),
                local(wv.at[span], wkb.at[d, :, pl.ds(HEAD, HEAD)], w_s.at[3 * d + 2]),
            )
        )

    greet([at(r, flip(t, d)) for d in (1, 2, 3)] + [at(flip(r, d), t) for d in (1, 2, 3)])
    m_copies = [
        send(meta, metas.at[d], (m_s, m_r), d - 1, at(flip(r, d), t)) for d in (1, 2, 3)
    ]
    tokens = LineGather(emb, lambda i: ebuf.at[i - 1], (e_s, e_r), at, r, t)
    kv_copy = send(
        cache, kv.at[pl.ds(par_dev, par_dev)], (k_s, k_r), 0, at(flip(r, 1), t)
    )
    kv_own = local(cache, kv.at[pl.ds(0, par_dev)], loc_s.at[0])
    metas[0] = table
    for copy in m_copies:
        copy.wait_recv()
    meta_copy = local(metas, meta_s, loc_s.at[1])
    out_loads = []
    for d in range(4):
        k = nth(t, d)
        out_loads.append(
            local(wo.at[pl.ds(pl.multiple_of(k * deep, deep), deep)], wob.at[d], wo_s.at[d])
        )
    meta_copy.wait()

    def parent_of(side, c):
        name = meta_s[2 * side, 0, 16 + c]
        owner = lax.div(name, par_dev)
        which = lax.rem(name, par_dev)
        away = jnp.where(lax.rem(owner, 2) == lax.rem(r, 2), 0, 1)
        other = jnp.where(lax.div(owner, 2) == lax.div(r, 2), 0, 1)
        return other == 0, away * par_dev + which, meta_s[2 * other + away, 0, which]

    step = lax.broadcasted_iota(jnp.int32, (steps, 128), 0)
    position = jnp.concatenate([parent_of(0, c)[2] + step for c in range(children)], axis=0)
    angle = position.astype(jnp.float32) * freq[...]
    cosine = jnp.cos(angle)
    half = lax.broadcasted_iota(jnp.int32, (rows, 128), 1) < HEAD // 2
    sine = jnp.sin(angle)
    sine = jnp.where(half, -sine, sine)

    squares = jnp.zeros((rows, 1), jnp.float32)
    for d in range(4):
        if d:
            tokens.arrived(d)
        block_in = emb[...] if d == 0 else ebuf[d - 1]
        whole = block_in.astype(jnp.float32)
        squares = squares + jnp.sum(whole * whole, axis=-1, keepdims=True)
        for load in loads[d]:
            load.wait()
        more_q = jnp.dot(block_in, wqb[d], preferred_element_type=jnp.float32)
        more_k = jnp.dot(block_in, wkb[d], preferred_element_type=jnp.float32)
        if d == 0:
            accq[...] = more_q
            acck[...] = more_k
        else:
            accq[...] += more_q
            acck[...] += more_k
    norm = lax.rsqrt(squares / (4 * width) + EPS)

    def turn(x):
        return x * cosine + pltpu.roll(x, HEAD // 2, 1) * sine

    def by_child(g, columns):
        heads[g] = columns * norm
        return jnp.concatenate(
            [heads[g, pl.ds(c, steps, stride=children), :] for c in range(children)], axis=0
        )

    def head_of(g):
        x = by_child(g, accq[:, g * HEAD : (g + 1) * HEAD])
        return turn(x).reshape(children, steps, HEAD)

    for j in range(GROUP // 2):
        pair = jnp.concatenate([head_of(2 * j), head_of(2 * j + 1)], axis=1)
        q_own[0, :, 2 * steps * j : 2 * steps * (j + 1), :] = pair.astype(jnp.bfloat16)

    partner = at(flip(r, 2), t)
    x_copies = [send(q_own.at[0], q_part.at[0], (x_s, x_r), 0, partner)]
    queries = LineGather(q_own.at[0], lambda i: q_own.at[i], (q_s, q_r), at, r, t)

    key_raw = by_child(GROUP, acck[:, :HEAD]).astype(jnp.bfloat16).astype(jnp.float32)
    key_new = turn(key_raw).astype(jnp.bfloat16)
    value = by_child(GROUP + 1, acck[:, HEAD:]).astype(jnp.bfloat16)
    total_rows = children * tall
    scores = (
        lax.dot_general(
            q_own[0].reshape(total_rows, HEAD),
            key_new,
            (((1,), (1,)), ((), ())),
            preferred_element_type=jnp.float32,
        )
        * SCALE
    )
    row = lax.broadcasted_iota(jnp.int32, (total_rows, rows), 0)
    col = lax.broadcasted_iota(jnp.int32, (total_rows, rows), 1)
    valid = (row // tall == col // steps) & (lax.rem(col, steps) <= lax.rem(row, steps))
    scores = jnp.where(valid, scores, NEG)
    top = jnp.max(scores, axis=-1, keepdims=True)
    weights = jnp.where(valid, jnp.exp(scores - top), 0.0)
    total = jnp.sum(weights, axis=-1, keepdims=True)
    summed = jnp.dot(weights.astype(jnp.bfloat16), value, preferred_element_type=jnp.float32)
    o_self[...] = (summed / total).reshape(children, tall, HEAD)
    l_self = compact(top + jnp.log(total), children, tall)

    kv_own.wait()
    kv_copy.wait_recv()
    column = lax.broadcasted_iota(jnp.int32, (tall, block), 1) + t * block
    lanes = lax.broadcasted_iota(jnp.int32, (tall, 128), 1)

    def attend(side, q, o_ref, head):
        first = pl.multiple_of(head * HEAD, HEAD)
        second = pl.multiple_of((KV_HEADS + head) * HEAD, HEAD)

        def some(i, lses):
            for u in range(UNROLL):
                c = i * UNROLL + u
                here, slot, length = parent_of(side, c)
                seen = jnp.logical_and(here, length > t * block)
                raw = lax.dot_general(
                    q[c],
                    kv[slot, :, pl.ds(first, HEAD)],
                    (((1,), (1,)), ((), ())),
                    preferred_element_type=jnp.float32,
                )
                raw = jnp.where(column < length, raw, NEG)
                peak = jnp.max(raw, axis=-1, keepdims=True)
                portion = jnp.exp2((raw - peak) * (SCALE * LOG2E))
                sums = jnp.sum(portion, axis=-1, keepdims=True)
                mixed = jnp.dot(
                    portion.astype(jnp.bfloat16),
                    kv[slot, :, pl.ds(second, HEAD)],
                    preferred_element_type=jnp.float32,
                )
                o_ref[c] = jnp.where(seen, mixed / sums, 0.0).astype(jnp.bfloat16)
                lse = jnp.where(seen, peak * SCALE + jnp.log(sums), NEG)
                lse = jnp.where(here, lse, 0.0)
                lses = jnp.where(lanes == c, lse, lses)
            return lses

        return lax.fori_loop(0, children // UNROLL, some, jnp.zeros((tall, 128), jnp.float32))

    r_copies = []
    t_copies = []

    def merge(d):
        for copy in r_copies[d]:
            copy.wait_recv()
        mo[d] = o_own[d] + rx_o[d]
        ml[d] = ml[d] + rx_l[d]
        if d:
            seat = 0 if d == 1 else 2 - lax.rem((t + 1) // 2, 2)
            device = at(r, nth(t, d))
            t_copies.append(
                (
                    send(mo.at[d], ao.at[seat], (zo_s, zo_r), d - 1, device, seat),
                    send(ml.at[d], al.at[seat], (zl_s, zl_r), d - 1, device, seat),
                )
            )

    def forward(d):
        queries.arrived(d)
        x_copies.append(send(q_own.at[d], q_part.at[d], (x_s, x_r), d, partner))

    for d in range(4):
        head = nth(t, d)
        ml[d] = attend(0, q_own.at[d], o_own.at[d], head)
        if d == 0:
            forward(1)
        x_copies[d].wait_recv()
        l_part[d] = attend(1, q_part.at[d], o_part.at[d], head)
        r_copies.append(
            (
                send(o_part.at[d], rx_o.at[d], (xo_s, xo_r), d, partner),
                send(l_part.at[d], rx_l.at[d], (xl_s, xl_r), d, partner),
            )
        )
        if d < 2:
            forward(d + 2)
        if d:
            merge(d - 1)
    merge(3)

    for seat in range(3):
        remote(ao.at[seat], ao.at[seat], (zo_s, zo_r), seat, partner).wait_recv()
        remote(al.at[seat], al.at[seat], (zl_s, zl_r), seat, partner).wait_recv()
    lses = [ml[0], l_self] + [al[d] for d in range(3)]
    top = functools.reduce(jnp.maximum, lses)
    shares = [jnp.exp(lse - top) for lse in lses]
    inverse = 1.0 / functools.reduce(jnp.add, shares)
    shares = [share * inverse for share in shares]
    for c in range(children):
        pieces = [mo[0, c], o_self[c]] + [ao[d, c] for d in range(3)]
        blend = jnp.zeros((tall, HEAD), jnp.float32)
        for share, piece in zip(shares, pieces):
            blend = blend + share[:, c : c + 1] * piece.astype(jnp.float32)
        for g in range(GROUP):
            heads[g, pl.ds(c, steps, stride=children), :] = blend[g * steps : (g + 1) * steps]
    for g in range(GROUP):
        att[:, g * HEAD : (g + 1) * HEAD] = heads[g].astype(jnp.bfloat16)
    blends = LineGather(att, lambda i: abuf.at[i - 1], (a_s, a_r), at, r, t)
    for d in range(4):
        if d:
            blends.arrived(d)
        block_in = att[...] if d == 0 else abuf[d - 1]
        out_loads[d].wait()
        more = jnp.dot(block_in, wob[d], preferred_element_type=jnp.float32)
        if d == 0:
            acc[...] = more
        elif d < 3:
            acc[...] += more
        else:
            out[...] = (acc[...] + more).astype(out.dtype)
    for copies in r_copies + t_copies:
        for copy in copies:
            copy.wait_send()
    for copy in m_copies + x_copies + [kv_copy]:
        copy.wait_send()
    for gather in (tokens, queries, blends):
        gather.finish()


def at_parents(embedded, w_query, w_key, w_value, w_out, prefix_cache, prefix_len, child_parent):
    steps, children, width = embedded.shape
    rows = steps * children
    par_dev, block, kv_width = prefix_cache.shape
    tall = GROUP * steps
    out_width = w_out.shape[1]
    bf16, f32, i32 = jnp.bfloat16, jnp.float32, jnp.int32
    any_space = pl.BlockSpec(memory_space=pl.ANY)
    vmem = pl.BlockSpec(memory_space=pltpu.VMEM)
    smem = pl.BlockSpec(memory_space=pltpu.SMEM)

    emb = embedded.reshape(rows, width)
    half = HEAD // 2
    freq = np.float32(ROPE_BASE) ** (-np.arange(half, dtype=np.float32) / np.float32(half))
    freq = jnp.asarray(np.concatenate([freq, freq])[None, :])

    def scratch(shape, kind=bf16):
        return pltpu.VMEM(shape, kind)

    result = pl.pallas_call(
        forked_kernel,
        out_shape=jax.ShapeDtypeStruct((rows, out_width), bf16),
        in_specs=[smem, smem, vmem, vmem] + [any_space] * 5,
        out_specs=vmem,
        scratch_shapes=[
            scratch((8, 128), i32),
            scratch((4, 8, 128), i32),
            pltpu.SMEM((4, 8, 128), i32),
            scratch((3, rows, width)),
            scratch((4, width, w_query.shape[1])),
            scratch((4, width, 2 * HEAD)),
            scratch((4, GROUP * HEAD, out_width)),
            scratch((rows, w_query.shape[1]), f32),
            scratch((rows, 2 * HEAD), f32),
            scratch((GROUP + 2, rows, HEAD), f32),
            scratch((2 * par_dev, block, kv_width)),
            scratch((4, children, tall, HEAD)),
            scratch((4, children, tall, HEAD)),
            scratch((4, children, tall, HEAD)),
            scratch((4, children, tall, HEAD)),
            scratch((4, tall, 128), f32),
            scratch((children, tall, HEAD), f32),
            scratch((4, children, tall, HEAD)),
            scratch((4, tall, 128), f32),
            scratch((4, children, tall, HEAD)),
            scratch((4, tall, 128), f32),
            scratch((3, children, tall, HEAD)),
            scratch((3, tall, 128), f32),
            scratch((rows, GROUP * HEAD)),
            scratch((3, rows, GROUP * HEAD)),
            scratch((rows, out_width), f32),
        ]
        + [
            pltpu.SemaphoreType.DMA((n,))
            for n in (5, 3, 12, 4, 5, 3, 4, 4, 3, 3, 1, 1, 2, 4, 4, 4, 4, 3, 3, 3, 3, 5, 3)
        ],
        compiler_params=pltpu.CompilerParams(
            collective_id=0, has_side_effects=True, vmem_limit_bytes=60 * 2**20
        ),
        name="forked",
    )(prefix_len, child_parent, emb, freq, w_query, w_key, w_value, w_out, prefix_cache)
    return result.reshape(steps, children, out_width)


def solution(mesh):
    in_specs = (
        P(None, ("parts", "replica"), "tensor"),
        P(None, "tensor"),
        P(None, "tensor"),
        P(None, "tensor"),
        P(None, "tensor"),
        P(("parts", "replica"), "tensor", None),
        P(("parts", "replica")),
        P(("parts", "replica")),
    )
    out_specs = P(None, ("parts", "replica"), "tensor")
    fits = mesh.shape["replica"] == 4 and mesh.shape["tensor"] == KV_HEADS
    body = at_parents if fits else per_device
    return jax.shard_map(
        body, mesh=mesh, in_specs=in_specs, out_specs=out_specs, check_vma=False
    )
```

```python
import functools

import jax
import jax.numpy as jnp
import numpy as np
from jax import lax
from jax.experimental import pallas as pl
from jax.experimental.pallas import tpu as pltpu
from jax.sharding import PartitionSpec as P

HEADS = 32
KV_HEADS = 4
HEAD = 128


EPS = 1e-06
NEG = -1e30
ROPE_BASE = 1000000.0


def combined_all(x, axis, combine):
    everything = jax.tree.map(
        lambda part, kind: lax.all_gather(part.astype(kind), axis),
        x,
        (jnp.bfloat16, jnp.bfloat16, jnp.bfloat16),
    )

    def take(k):
        return jax.tree.map(lambda part, own: part[k].astype(own.dtype), everything, x)

    return lax.fori_loop(
        1, lax.axis_size(axis), lambda k, so_far: combine(so_far, take(k)), take(0)
    )


def rotate(values, positions):
    half = values.shape[-1] // 2
    freq = ROPE_BASE ** (-jnp.arange(half, dtype=jnp.float32) / half)
    angle = positions.astype(jnp.float32)[..., None] * freq
    cosine = jnp.cos(angle)
    sine = jnp.sin(angle)
    first = values[..., :half]
    second = values[..., half:]
    return jnp.concatenate(
        [first * cosine - second * sine, first * sine + second * cosine], axis=-1
    )


def combine(first, second):
    upper = jnp.maximum(first[0], second[0])
    left = jnp.exp(first[0] - upper)
    right = jnp.exp(second[0] - upper)
    return (
        upper,
        first[1] * left + second[1] * right,
        first[2] * left[..., None] + second[2] * right[..., None],
    )


def rms_normed(current):
    whole = current.astype(jnp.float32)
    return (whole * lax.rsqrt(jnp.mean(whole * whole, axis=-1, keepdims=True) + EPS)).astype(
        jnp.bfloat16
    )


def per_device(embedded, w_query, w_key, w_value, w_out, prefix_cache, prefix_len, child_parent):
    steps = embedded.shape[0]
    rows = embedded.shape[1]
    par_dev, pos_dev, width = prefix_cache.shape
    kv_width = width // 2
    group = HEADS // KV_HEADS
    scale = HEAD ** (-0.5)
    table = lax.all_gather(prefix_cache, "replica", axis=0, tiled=True)
    lengths_all = lax.all_gather(prefix_len, "replica", axis=0, tiled=True)
    lengths = lengths_all[child_parent]
    chosen = jnp.take(table, child_parent, axis=0)
    keys = jnp.transpose(
        chosen[:, :, :kv_width].reshape(rows, pos_dev, KV_HEADS, HEAD), (0, 2, 1, 3)
    )
    values = jnp.transpose(
        chosen[:, :, kv_width:].reshape(rows, pos_dev, KV_HEADS, HEAD), (0, 2, 1, 3)
    )
    positions = lax.axis_index("tensor") * pos_dev + jnp.arange(pos_dev, dtype=jnp.int32)
    valid = positions[None, :] < lengths[:, None]
    block_mask = valid[:, None, None, :]
    features = jnp.stack(
        [lax.all_gather(embedded[step], "tensor", axis=1, tiled=True) for step in range(steps)],
        axis=0,
    )
    normed = rms_normed(features).reshape(steps * rows, -1)
    position = lengths[None, :] + jnp.arange(steps, dtype=jnp.int32)[:, None]
    query_part = jnp.dot(normed, w_query, preferred_element_type=jnp.float32)
    local_heads = query_part.shape[1] // HEAD
    query_part = (
        rotate(query_part.reshape(steps, rows, local_heads, HEAD), position[:, :, None])
        .reshape(steps, rows, local_heads * HEAD)
        .astype(jnp.bfloat16)
    )
    key_part = (
        jnp.dot(normed, w_key, preferred_element_type=jnp.float32)
        .astype(jnp.bfloat16)
        .reshape(steps, rows, -1)
    )
    value_part = (
        jnp.dot(normed, w_value, preferred_element_type=jnp.float32)
        .astype(jnp.bfloat16)
        .reshape(steps, rows, -1)
    )
    query_all, key_all, value_all = (
        lax.all_gather(query_part, "tensor", axis=2, tiled=True),
        lax.all_gather(key_part, "tensor", axis=2, tiled=True),
        lax.all_gather(value_part, "tensor", axis=2, tiled=True),
    )
    own_keys = rotate(
        key_all.astype(jnp.float32).reshape(steps, rows, KV_HEADS, HEAD), position[:, :, None]
    ).astype(jnp.bfloat16)
    own_values = value_all.reshape(steps, rows, KV_HEADS, HEAD)
    queries = query_all.reshape(steps, rows, KV_HEADS, group, HEAD)
    scores = (
        jnp.einsum("sckgd,ckpd->sckgp", queries, keys, preferred_element_type=jnp.float32) * scale
    )
    full_mask = block_mask[None]
    scores = jnp.where(full_mask, scores, NEG)
    upper = jnp.max(scores, axis=-1)
    weights = jnp.where(full_mask, jnp.exp(scores - upper[..., None]), 0.0)
    total = jnp.sum(weights, axis=-1)
    partial_value = jnp.einsum(
        "sckgp,ckpd->sckgd",
        weights.astype(jnp.bfloat16),
        values,
        preferred_element_type=jnp.float32,
    )
    merged = combined_all((upper, total, partial_value), "tensor", combine)
    causal = (jnp.arange(steps)[None, :] <= jnp.arange(steps)[:, None])[:, None, None, None, :]
    own_scores = (
        jnp.einsum("sckgd,tckd->sckgt", queries, own_keys, preferred_element_type=jnp.float32)
        * scale
    )
    own_scores = jnp.where(causal, own_scores, NEG)
    own_upper = jnp.max(own_scores, axis=-1)
    own_weights = jnp.where(causal, jnp.exp(own_scores - own_upper[..., None]), 0.0)
    own_total = jnp.sum(own_weights, axis=-1)
    own_partial = jnp.einsum(
        "sckgt,tckd->sckgd",
        own_weights.astype(jnp.bfloat16),
        own_values,
        preferred_element_type=jnp.float32,
    )
    final = combine(merged, (own_upper, own_total, own_partial))
    attended = (
        (final[2] / final[1][..., None]).reshape(steps * rows, HEADS * HEAD).astype(jnp.bfloat16)
    )
    result = jnp.dot(attended, w_out, preferred_element_type=jnp.float32).astype(jnp.bfloat16)
    return result.reshape(steps, rows, -1)


GROUP = HEADS // KV_HEADS
SCALE = HEAD ** (-0.5)
LOG2E = 1.4426950408889634
UNROLL = 4
MESH = pl.DeviceIdType.MESH


def flip(index, step):
    if step == 0:
        return index
    if step == 1:
        return index + 1 - 2 * lax.rem(index, 2)
    if step == 2:
        return index + 2 - 4 * (index // 2)
    return 3 - index


def remote(src, dst, sems, slot, device, landing=None):
    return pltpu.make_async_remote_copy(
        src_ref=src,
        dst_ref=dst,
        send_sem=sems[0].at[slot],
        recv_sem=sems[1].at[slot if landing is None else landing],
        device_id=device,
        device_id_type=MESH,
    )


def send(*args):
    copy = remote(*args)
    copy.start()
    return copy


def nth(t, i):
    return (t, flip(t, 1), 2 - t // 2, 3 - 3 * (t // 2))[i]


class LineGather:
    def __init__(self, own, slots, sems, at, r, t):
        self.middle = lax.rem((t + 1) // 2, 2) == 1
        end, other = at(r, flip(t, 1)), at(r, 3 - t)
        plan = (
            (own, 1, end),
            (own, 2, other),
            (slots(1), 3, other),
            (slots(2), 2, end),
            (slots(3), 3, end),
        )
        self.copies = [
            remote(src, slots(to), sems, n, device, to - 1)
            for n, (src, to, device) in enumerate(plan)
        ]
        self.landings = [remote(slots(i), slots(i), sems, 0, end, i - 1) for i in (1, 2, 3)]
        self.copies[0].start()
        self.if_middle(self.copies[1].start)

    def if_middle(self, act):
        @pl.when(self.middle)
        def _():
            act()

    def arrived(self, i):
        self.landings[i - 1].wait_recv()
        self.if_middle(self.copies[i + 1].start)

    def finish(self):
        self.copies[0].wait_send()

        @pl.when(self.middle)
        def _():
            for copy in self.copies[1:]:
                copy.wait_send()


def greet(devices):
    barrier = pltpu.get_barrier_semaphore()
    for device in devices:
        pl.semaphore_signal(barrier, inc=1, device_id=device, device_id_type=MESH)
    pl.semaphore_wait(barrier, len(devices))


def compact(column, children, rows):
    lane = lax.broadcasted_iota(jnp.int32, (rows, 128), 1)
    out = jnp.zeros((rows, 128), jnp.float32)
    for c in range(children):
        out = jnp.where(lane == c, column[c * rows : (c + 1) * rows], out)
    return out


def forked_kernel(
    lens,
    names,
    emb,
    freq,
    wq,
    wk,
    wv,
    wo,
    cache,
    out,
    meta,
    metas,
    meta_s,
    ebuf,
    wqb,
    wkb,
    wob,
    accq,
    acck,
    heads,
    kv,
    q_own,
    q_part,
    o_own,
    o_part,
    l_part,
    o_self,
    rx_o,
    rx_l,
    mo,
    ml,
    ao,
    al,
    att,
    abuf,
    acc,
    e_s,
    e_r,
    w_s,
    wo_s,
    q_s,
    q_r,
    x_s,
    x_r,
    m_s,
    m_r,
    k_s,
    k_r,
    loc_s,
    xo_s,
    xo_r,
    xl_s,
    xl_r,
    zo_s,
    zo_r,
    zl_s,
    zl_r,
    a_s,
    a_r,
):
    part = lax.axis_index("parts")
    r = lax.axis_index("replica")
    t = lax.axis_index("tensor")
    rows, width = emb.shape
    children, tall = q_own.shape[1], q_own.shape[2]
    steps = rows // children
    par_dev, block = cache.shape[0], cache.shape[1]
    deep = GROUP * HEAD

    def at(rep, ten):
        return (part, rep, ten)

    def local(src, dst, sem):
        copy = pltpu.make_async_copy(src, dst, sem)
        copy.start()
        return copy

    lane = lax.broadcasted_iota(jnp.int32, (8, 128), 1)
    table = jnp.zeros((8, 128), jnp.int32)
    for i in range(par_dev):
        table = jnp.where(lane == i, lens[i], table)
    for c in range(children):
        table = jnp.where(lane == 16 + c, names[c], table)
    meta[...] = table

    loads = []
    for d in range(4):
        k = nth(t, d)
        span = pl.ds(pl.multiple_of(k * width, width), width)
        loads.append(
            (
                local(wq.at[span], wqb.at[d], w_s.at[3 * d]),
                local(wk.at[span], wkb.at[d, :, pl.ds(0, HEAD)], w_s.at[3 * d + 1]),
                local(wv.at[span], wkb.at[d, :, pl.ds(HEAD, HEAD)], w_s.at[3 * d + 2]),
            )
        )

    greet([at(r, flip(t, d)) for d in (1, 2, 3)] + [at(flip(r, d), t) for d in (1, 2, 3)])
    m_copies = [
        send(meta, metas.at[d], (m_s, m_r), d - 1, at(flip(r, d), t)) for d in (1, 2, 3)
    ]
    tokens = LineGather(emb, lambda i: ebuf.at[i - 1], (e_s, e_r), at, r, t)
    kv_copy = send(
        cache, kv.at[pl.ds(par_dev, par_dev)], (k_s, k_r), 0, at(flip(r, 1), t)
    )
    kv_own = local(cache, kv.at[pl.ds(0, par_dev)], loc_s.at[0])
    metas[0] = table
    for copy in m_copies:
        copy.wait_recv()
    meta_copy = local(metas, meta_s, loc_s.at[1])
    out_loads = []
    for d in range(4):
        k = nth(t, d)
        out_loads.append(
            local(wo.at[pl.ds(pl.multiple_of(k * deep, deep), deep)], wob.at[d], wo_s.at[d])
        )
    meta_copy.wait()

    def parent_of(side, c):
        name = meta_s[2 * side, 0, 16 + c]
        owner = lax.div(name, par_dev)
        which = lax.rem(name, par_dev)
        away = jnp.where(lax.rem(owner, 2) == lax.rem(r, 2), 0, 1)
        other = jnp.where(lax.div(owner, 2) == lax.div(r, 2), 0, 1)
        return other == 0, away * par_dev + which, meta_s[2 * other + away, 0, which]

    step = lax.broadcasted_iota(jnp.int32, (steps, 128), 0)
    position = jnp.concatenate([parent_of(0, c)[2] + step for c in range(children)], axis=0)
    angle = position.astype(jnp.float32) * freq[...]
    cosine = jnp.cos(angle)
    half = lax.broadcasted_iota(jnp.int32, (rows, 128), 1) < HEAD // 2
    sine = jnp.sin(angle)
    sine = jnp.where(half, -sine, sine)

    squares = jnp.zeros((rows, 1), jnp.float32)
    for d in range(4):
        if d:
            tokens.arrived(d)
        block_in = emb[...] if d == 0 else ebuf[d - 1]
        whole = block_in.astype(jnp.float32)
        squares = squares + jnp.sum(whole * whole, axis=-1, keepdims=True)
        for load in loads[d]:
            load.wait()
        more_q = jnp.dot(block_in, wqb[d], preferred_element_type=jnp.float32)
        more_k = jnp.dot(block_in, wkb[d], preferred_element_type=jnp.float32)
        if d == 0:
            accq[...] = more_q
            acck[...] = more_k
        else:
            accq[...] += more_q
            acck[...] += more_k
    norm = lax.rsqrt(squares / (4 * width) + EPS)

    def turn(x):
        return x * cosine + pltpu.roll(x, HEAD // 2, 1) * sine

    def by_child(g, columns):
        heads[g] = columns * norm
        return jnp.concatenate(
            [heads[g, pl.ds(c, steps, stride=children), :] for c in range(children)], axis=0
        )

    def head_of(g):
        x = by_child(g, accq[:, g * HEAD : (g + 1) * HEAD])
        return turn(x).reshape(children, steps, HEAD)

    for j in range(GROUP // 2):
        pair = jnp.concatenate([head_of(2 * j), head_of(2 * j + 1)], axis=1)
        q_own[0, :, 2 * steps * j : 2 * steps * (j + 1), :] = pair.astype(jnp.bfloat16)

    partner = at(flip(r, 2), t)
    x_copies = [send(q_own.at[0], q_part.at[0], (x_s, x_r), 0, partner)]
    queries = LineGather(q_own.at[0], lambda i: q_own.at[i], (q_s, q_r), at, r, t)

    key_raw = by_child(GROUP, acck[:, :HEAD]).astype(jnp.bfloat16).astype(jnp.float32)
    key_new = turn(key_raw).astype(jnp.bfloat16)
    value = by_child(GROUP + 1, acck[:, HEAD:]).astype(jnp.bfloat16)
    total_rows = children * tall
    scores = (
        lax.dot_general(
            q_own[0].reshape(total_rows, HEAD),
            key_new,
            (((1,), (1,)), ((), ())),
            preferred_element_type=jnp.float32,
        )
        * SCALE
    )
    row = lax.broadcasted_iota(jnp.int32, (total_rows, rows), 0)
    col = lax.broadcasted_iota(jnp.int32, (total_rows, rows), 1)
    valid = (row // tall == col // steps) & (lax.rem(col, steps) <= lax.rem(row, steps))
    scores = jnp.where(valid, scores, NEG)
    top = jnp.max(scores, axis=-1, keepdims=True)
    weights = jnp.where(valid, jnp.exp(scores - top), 0.0)
    total = jnp.sum(weights, axis=-1, keepdims=True)
    summed = jnp.dot(weights.astype(jnp.bfloat16), value, preferred_element_type=jnp.float32)
    o_self[...] = (summed / total).reshape(children, tall, HEAD)
    l_self = compact(top + jnp.log(total), children, tall)

    kv_own.wait()
    kv_copy.wait_recv()
    column = lax.broadcasted_iota(jnp.int32, (tall, block), 1) + t * block
    lanes = lax.broadcasted_iota(jnp.int32, (tall, 128), 1)

    def attend(side, q, o_ref, head):
        first = pl.multiple_of(head * HEAD, HEAD)
        second = pl.multiple_of((KV_HEADS + head) * HEAD, HEAD)

        def some(i, lses):
            for u in range(UNROLL):
                c = i * UNROLL + u
                here, slot, length = parent_of(side, c)
                seen = jnp.logical_and(here, length > t * block)
                raw = lax.dot_general(
                    q[c],
                    kv[slot, :, pl.ds(first, HEAD)],
                    (((1,), (1,)), ((), ())),
                    preferred_element_type=jnp.float32,
                )
                raw = jnp.where(column < length, raw, NEG)
                peak = jnp.max(raw, axis=-1, keepdims=True)
                portion = jnp.exp2((raw - peak) * (SCALE * LOG2E))
                sums = jnp.sum(portion, axis=-1, keepdims=True)
                mixed = jnp.dot(
                    portion.astype(jnp.bfloat16),
                    kv[slot, :, pl.ds(second, HEAD)],
                    preferred_element_type=jnp.float32,
                )
                o_ref[c] = jnp.where(seen, mixed / sums, 0.0).astype(jnp.bfloat16)
                lse = jnp.where(seen, peak * SCALE + jnp.log(sums), NEG)
                lse = jnp.where(here, lse, 0.0)
                lses = jnp.where(lanes == c, lse, lses)
            return lses

        return lax.fori_loop(0, children // UNROLL, some, jnp.zeros((tall, 128), jnp.float32))

    r_copies = {}
    t_copies = []

    def merge(d):
        for copy in r_copies[d]:
            copy.wait_recv()
        mo[d] = o_own[d] + rx_o[d]
        ml[d] = ml[d] + rx_l[d]
        if d:
            seat = 0 if d == 1 else 2 - lax.rem((t + 1) // 2, 2)
            device = at(r, nth(t, d))
            t_copies.append(
                (
                    send(mo.at[d], ao.at[seat], (zo_s, zo_r), d - 1, device, seat),
                    send(ml.at[d], al.at[seat], (zl_s, zl_r), d - 1, device, seat),
                )
            )

    def forward(d):
        queries.arrived(d)
        x_copies.append(send(q_own.at[d], q_part.at[d], (x_s, x_r), d, partner))

    def own_side(d):
        ml[d] = attend(0, q_own.at[d], o_own.at[d], nth(t, d))

    def partner_side(d):
        l_part[d] = attend(1, q_part.at[d], o_part.at[d], nth(t, d))
        r_copies[d] = (
            send(o_part.at[d], rx_o.at[d], (xo_s, xo_r), d, partner),
            send(l_part.at[d], rx_l.at[d], (xl_s, xl_r), d, partner),
        )

    own_side(0)
    forward(1)
    own_side(1)
    x_copies[1].wait_recv()
    forward(2)
    partner_side(1)
    own_side(2)
    x_copies[2].wait_recv()
    forward(3)
    partner_side(2)
    own_side(3)
    merge(1)
    x_copies[3].wait_recv()
    partner_side(3)
    x_copies[0].wait_recv()
    partner_side(0)
    merge(2)
    merge(3)
    merge(0)

    for seat in range(3):
        remote(ao.at[seat], ao.at[seat], (zo_s, zo_r), seat, partner).wait_recv()
        remote(al.at[seat], al.at[seat], (zl_s, zl_r), seat, partner).wait_recv()
    lses = [ml[0], l_self] + [al[d] for d in range(3)]
    top = functools.reduce(jnp.maximum, lses)
    shares = [jnp.exp(lse - top) for lse in lses]
    inverse = 1.0 / functools.reduce(jnp.add, shares)
    shares = [share * inverse for share in shares]
    for c in range(children):
        pieces = [mo[0, c], o_self[c]] + [ao[d, c] for d in range(3)]
        blend = jnp.zeros((tall, HEAD), jnp.float32)
        for share, piece in zip(shares, pieces):
            blend = blend + share[:, c : c + 1] * piece.astype(jnp.float32)
        for g in range(GROUP):
            heads[g, pl.ds(c, steps, stride=children), :] = blend[g * steps : (g + 1) * steps]
    for g in range(GROUP):
        att[:, g * HEAD : (g + 1) * HEAD] = heads[g].astype(jnp.bfloat16)
    blends = LineGather(att, lambda i: abuf.at[i - 1], (a_s, a_r), at, r, t)
    for d in range(4):
        if d:
            blends.arrived(d)
        block_in = att[...] if d == 0 else abuf[d - 1]
        out_loads[d].wait()
        more = jnp.dot(block_in, wob[d], preferred_element_type=jnp.float32)
        if d == 0:
            acc[...] = more
        elif d < 3:
            acc[...] += more
        else:
            out[...] = (acc[...] + more).astype(out.dtype)
    for copies in list(r_copies.values()) + t_copies:
        for copy in copies:
            copy.wait_send()
    for copy in m_copies + x_copies + [kv_copy]:
        copy.wait_send()
    for gather in (tokens, queries, blends):
        gather.finish()


def at_parents(embedded, w_query, w_key, w_value, w_out, prefix_cache, prefix_len, child_parent):
    steps, children, width = embedded.shape
    rows = steps * children
    par_dev, block, kv_width = prefix_cache.shape
    tall = GROUP * steps
    out_width = w_out.shape[1]
    bf16, f32, i32 = jnp.bfloat16, jnp.float32, jnp.int32
    any_space = pl.BlockSpec(memory_space=pl.ANY)
    vmem = pl.BlockSpec(memory_space=pltpu.VMEM)
    smem = pl.BlockSpec(memory_space=pltpu.SMEM)

    emb = embedded.reshape(rows, width)
    half = HEAD // 2
    freq = np.float32(ROPE_BASE) ** (-np.arange(half, dtype=np.float32) / np.float32(half))
    freq = jnp.asarray(np.concatenate([freq, freq])[None, :])

    def scratch(shape, kind=bf16):
        return pltpu.VMEM(shape, kind)

    result = pl.pallas_call(
        forked_kernel,
        out_shape=jax.ShapeDtypeStruct((rows, out_width), bf16),
        in_specs=[smem, smem, vmem, vmem] + [any_space] * 5,
        out_specs=vmem,
        scratch_shapes=[
            scratch((8, 128), i32),
            scratch((4, 8, 128), i32),
            pltpu.SMEM((4, 8, 128), i32),
            scratch((3, rows, width)),
            scratch((4, width, w_query.shape[1])),
            scratch((4, width, 2 * HEAD)),
            scratch((4, GROUP * HEAD, out_width)),
            scratch((rows, w_query.shape[1]), f32),
            scratch((rows, 2 * HEAD), f32),
            scratch((GROUP + 2, rows, HEAD), f32),
            scratch((2 * par_dev, block, kv_width)),
            scratch((4, children, tall, HEAD)),
            scratch((4, children, tall, HEAD)),
            scratch((4, children, tall, HEAD)),
            scratch((4, children, tall, HEAD)),
            scratch((4, tall, 128), f32),
            scratch((children, tall, HEAD), f32),
            scratch((4, children, tall, HEAD)),
            scratch((4, tall, 128), f32),
            scratch((4, children, tall, HEAD)),
            scratch((4, tall, 128), f32),
            scratch((3, children, tall, HEAD)),
            scratch((3, tall, 128), f32),
            scratch((rows, GROUP * HEAD)),
            scratch((3, rows, GROUP * HEAD)),
            scratch((rows, out_width), f32),
        ]
        + [
            pltpu.SemaphoreType.DMA((n,))
            for n in (5, 3, 12, 4, 5, 3, 4, 4, 3, 3, 1, 1, 2, 4, 4, 4, 4, 3, 3, 3, 3, 5, 3)
        ],
        compiler_params=pltpu.CompilerParams(
            collective_id=0, has_side_effects=True, vmem_limit_bytes=60 * 2**20
        ),
        name="forked",
    )(prefix_len, child_parent, emb, freq, w_query, w_key, w_value, w_out, prefix_cache)
    return result.reshape(steps, children, out_width)


def solution(mesh):
    in_specs = (
        P(None, ("parts", "replica"), "tensor"),
        P(None, "tensor"),
        P(None, "tensor"),
        P(None, "tensor"),
        P(None, "tensor"),
        P(("parts", "replica"), "tensor", None),
        P(("parts", "replica")),
        P(("parts", "replica")),
    )
    out_specs = P(None, ("parts", "replica"), "tensor")
    fits = mesh.shape["replica"] == 4 and mesh.shape["tensor"] == KV_HEADS
    body = at_parents if fits else per_device
    return jax.shard_map(
        body, mesh=mesh, in_specs=in_specs, out_specs=out_specs, check_vma=False
    )
```
